128 devices in a mesh: ctx: 64 (over z, x, y_lo, core), head: 2 (over y_hi).
Axes of the slice: x: 4, y: 4 (y_hi: 2, y_lo: 2; y = y_hi * 2 + y_lo), z: 4, core: 2. Of those that a mesh axis runs over, the one named last changes fastest.
Arguments:
- frames: bfloat16 [8192, 768], P('ctx'), as said below
- tangent: bfloat16 [8192, 768], P('ctx'), may hold values from -6 to 6
- norm_gain: float32 [768], replicated, may hold values from 0.25 to 1.75
- query_weight: bfloat16 [768, 768], P(None, 'head'), as said below
- key_weight: bfloat16 [768, 768], P(None, 'head'), as said below
- value_weight: bfloat16 [768, 768], P(None, 'head'), may hold values from -0.21875 to 0.21875
- out_weight: bfloat16 [768, 768], P('head'), may hold values from -0.21875 to 0.21875
- conv_weight: float32 [31, 768], replicated, may hold values from -1 to 1
- conv_bias: float32 [768], replicated, may hold values from -3 to 3
- mix_weight: bfloat16 [768, 768], P(None, 'head'), may hold values from -0.21875 to 0.21875
Outputs:
- layer_out: bfloat16 [8192, 768], P('ctx', 'head')
- layer_slope: bfloat16 [8192, 768], P('ctx', 'head')
The draws below stay inside these ranges and needn't reach their ends.
Inputs may be any that keep to these rules, and one draw needn't show every extreme that they name: Latent frames. `query_weight`: a projection matrix. `key_weight`: a projection matrix.
All inputs are finite; a program needn't handle non-finite values.
Results may differ from the reference program's by a relative error of at most 0.04.
The reference program's roundings to bfloat16 on the way (of `normed`, `normed_slope`, `queries`, `rounded`, `heads_slope`, `mixed` and `active`) count: a program that leaves them out, or rounds other values in their place, can miss the bound.
Values may be sent and summed in bfloat16 or wider, within the bound.
A program may use at most 128 MiB of HBM per device.

```python
import math
import jax
import jax.numpy as jnp
from jax import lax

HEADS = 12
HDIM = 64
D = 768
TAPS = 31
FRAMES = 8192


def draw_query_weight(key, part):
    key = jax.random.fold_in(key, 1)
    jitter = jax.random.normal(key, (D, D), jnp.float32)
    matrix = jitter
    return (matrix / math.sqrt(D)).astype(jnp.bfloat16)


def draw_key_weight(key, part):
    key = jax.random.fold_in(key, 2)
    jitter = jax.random.normal(key, (D, D), jnp.float32)
    matrix = jitter
    return (matrix / math.sqrt(D)).astype(jnp.bfloat16)


def draw_frames(key, part):
    key = jax.random.fold_in(key, 3)
    matrix = jax.random.normal(key, (FRAMES, D), jnp.float32)
    return jnp.clip(matrix, -6.0, 6.0).astype(jnp.bfloat16)


def levels(rng, dims, shards, low, top_value):
    gain = 1.0
    for dim, parts in shards:
        heights = jax.random.uniform(jax.random.fold_in(jax.random.fold_in(rng, 6), dim), (parts,), jnp.float32, low / len(shards), top_value / len(shards))
        gain = gain * jnp.repeat(jnp.exp(heights), dims[dim] // parts).reshape((-1,) + (1,) * (len(dims) - 1 - dim))
    return gain


def scatter_about(rng, extent, deviation, most, shards=(), held_as=jnp.bfloat16):
    drawn = deviation * jax.random.normal(rng, extent, jnp.float32)
    if shards:
        drawn = drawn * levels(rng, extent, shards, -0.22, 0.18)
    return jnp.clip(drawn, -most, most).astype(held_as)


def setup_inputs(seed: int = 0) -> dict:
    seeds = jax.random.split(jax.random.key(seed), 11)
    frames = draw_frames(jax.random.fold_in(seeds[10], 71), 0)
    tangent = scatter_about(seeds[1], (FRAMES, D), 1.0, 6.0, ((0, 64),))
    norm_gain = jnp.clip(1.0 + 0.15 * jax.random.normal(seeds[2], (D,), jnp.float32), 0.25, 1.75)
    query_weight = draw_query_weight(jax.random.fold_in(seeds[10], 71), 0)
    key_weight = draw_key_weight(jax.random.fold_in(seeds[10], 71), 0)
    value_weight = scatter_about(seeds[5], (D, D), D ** -0.5, 0.21875, ((1, 2),))
    out_weight = scatter_about(seeds[6], (D, D), D ** -0.5, 0.21875, ((0, 2),))
    conv_weight = scatter_about(seeds[7], (TAPS, D), TAPS ** -0.5, 1.0, (), jnp.float32)
    conv_bias = scatter_about(seeds[8], (D,), 0.5, 3.0, (), jnp.float32)
    mix_weight = scatter_about(seeds[9], (D, D), D ** -0.5, 0.21875, ((1, 2),))
    return dict(frames=frames, tangent=tangent, norm_gain=norm_gain, query_weight=query_weight, key_weight=key_weight, value_weight=value_weight, out_weight=out_weight, conv_weight=conv_weight, conv_bias=conv_bias, mix_weight=mix_weight)


epsilon = 1e-06

def normalize(frames, tangent, norm_gain):
    plain_rows = frames.astype(jnp.float32)
    slope_rows = tangent.astype(jnp.float32)
    mean_square = lax.optimization_barrier(jnp.mean(plain_rows * plain_rows, axis=-1, keepdims=True))
    inverse = lax.rsqrt(mean_square + epsilon)
    cross_mean = lax.optimization_barrier(jnp.mean(plain_rows * slope_rows, axis=-1, keepdims=True))
    normed = (plain_rows * inverse * norm_gain).astype(jnp.bfloat16)
    normed_slope = (norm_gain * (slope_rows * inverse - plain_rows * inverse * inverse * inverse * cross_mean)).astype(jnp.bfloat16)
    return (normed, normed_slope)

def widen(matrix):
    return lax.optimization_barrier(matrix.astype(jnp.bfloat16)).astype(jnp.float32)

def attend_block(pieces, key_rows, pair_keys, value_rows, value_slope):
    queries, pair_queries = pieces
    score_scale = 1.0 / math.sqrt(HDIM)
    scores = jnp.einsum('qhd,khd->hqk', queries, key_rows) * score_scale
    slopes = jnp.einsum('qhd,khd->hqk', pair_queries, pair_keys) * score_scale
    weights = jnp.exp(scores - lax.optimization_barrier(jnp.max(scores, axis=-1, keepdims=True)))
    totals = lax.optimization_barrier(jnp.sum(weights, axis=-1))
    moments = lax.optimization_barrier(jnp.sum(weights * slopes, axis=-1))
    rounded = widen(weights)
    slanted = widen(weights * slopes)
    summed_out = jnp.einsum('hqk,khd->hqd', rounded, value_rows)
    summed_slope = jnp.einsum('hqk,khd->hqd', slanted, value_rows) + jnp.einsum('hqk,khd->hqd', rounded, value_slope)
    attended = summed_out / totals[..., None]
    attended_slope = summed_slope / totals[..., None] - (moments / totals)[..., None] * attended
    return (attended.transpose(1, 0, 2).astype(jnp.bfloat16), attended_slope.transpose(1, 0, 2).astype(jnp.bfloat16))

def reference(frames, tangent, norm_gain, query_weight, key_weight, value_weight, out_weight, conv_weight, conv_bias, mix_weight):
    normed, normed_slope = normalize(frames, tangent, norm_gain)

    def project(weight):
        return (jnp.dot(normed, weight, preferred_element_type=jnp.float32).astype(jnp.bfloat16), jnp.dot(normed_slope, weight, preferred_element_type=jnp.float32).astype(jnp.bfloat16))

    def split_heads(matrix):
        return matrix.astype(jnp.float32).reshape(FRAMES, HEADS, HDIM)
    queries, query_slope = project(query_weight)
    key_rows, key_slope = project(key_weight)
    value_rows, value_slope = project(value_weight)
    pair_queries = jnp.concatenate([split_heads(queries), split_heads(query_slope)], axis=-1)
    pair_keys = jnp.concatenate([split_heads(key_slope), split_heads(key_rows)], axis=-1)
    block_rows = min(256, FRAMES)
    count = FRAMES // block_rows
    blocked = (split_heads(queries).reshape(count, block_rows, HEADS, HDIM), pair_queries.reshape(count, block_rows, HEADS, 2 * HDIM))
    keys_wide = split_heads(key_rows)
    values_wide = split_heads(value_rows)
    values_slope_wide = split_heads(value_slope)
    out_blocks, slope_blocks = lax.map(lambda pieces: attend_block(pieces, keys_wide, pair_keys, values_wide, values_slope_wide), blocked)
    heads_out = out_blocks.reshape(FRAMES, D)
    heads_slope = slope_blocks.reshape(FRAMES, D)
    mixed = (frames.astype(jnp.float32) + jnp.dot(heads_out, out_weight, preferred_element_type=jnp.float32)).astype(jnp.bfloat16)
    mixed_slope = (tangent.astype(jnp.float32) + jnp.dot(heads_slope, out_weight, preferred_element_type=jnp.float32)).astype(jnp.bfloat16)
    margin = TAPS // 2
    plain_rows = mixed.astype(jnp.float32)
    slope_rows = mixed_slope.astype(jnp.float32)
    preact = jnp.zeros((FRAMES, D), jnp.float32)
    filtered_slope = jnp.zeros((FRAMES, D), jnp.float32)
    for tap_index in range(TAPS):
        preact = preact + conv_weight[tap_index] * jnp.roll(plain_rows, margin - tap_index, axis=0)
        filtered_slope = filtered_slope + conv_weight[tap_index] * jnp.roll(slope_rows, margin - tap_index, axis=0)
    preact = preact + conv_bias
    gating = jax.nn.sigmoid(preact)
    active = (preact * gating).astype(jnp.bfloat16)
    active_slope = (gating * (1.0 + preact * (1.0 - gating)) * filtered_slope).astype(jnp.bfloat16)
    layer_out = (plain_rows + jnp.dot(active, mix_weight, preferred_element_type=jnp.float32)).astype(jnp.bfloat16)
    layer_slope = (slope_rows + jnp.dot(active_slope, mix_weight, preferred_element_type=jnp.float32)).astype(jnp.bfloat16)
    return (layer_out, layer_slope)
```

```python
import functools

import jax
import jax.numpy as jnp
from jax import lax
from jax.experimental import pallas as pl
from jax.experimental.pallas import tpu as pltpu
from jax.sharding import PartitionSpec as P

MESH = pl.DeviceIdType.MESH
HDIM = 64
EPSILON = 1e-06
ROWS = 128
STAT = 16
MARGIN = 16
FACTORS = {64: (4, 4, 2, 2), 8: (2, 2, 1, 2)}


def split3(value):
    first = value.astype(jnp.bfloat16)
    rest = value - first.astype(jnp.float32)
    second = rest.astype(jnp.bfloat16)
    third = (rest - second.astype(jnp.float32)).astype(jnp.bfloat16)
    return [first, second, third]


def kernel(
    sizes,
    heads,
    frames_ref,
    tangent_ref,
    gain_ref,
    wq_ref,
    wk_ref,
    wv_ref,
    wo_ref,
    taps_ref,
    bias_ref,
    wm_ref,
    out_ref,
    slope_ref,
    kv,
    qq,
    part_out,
    part_in,
    joined,
    wo_far,
    padded,
    wide,
    act,
    kv_send,
    kv_recv,
    q_send,
    q_recv,
    part_send,
    part_recv,
    head_send,
    head_recv,
    wo_sem,
    halo_sem,
    act_send,
    act_recv,
):
    zs, xs, ys, cs = sizes
    nk, nq = xs * cs, zs * ys
    count = zs * xs * ys * cs
    half = heads * HDIM
    me = lax.axis_index("ctx")
    group = lax.axis_index("head")
    core = lax.rem(me, cs)
    yl = lax.rem(me // cs, ys)
    x = lax.rem(me // (cs * ys), xs)
    z = me // (cs * ys * xs)
    my_k = x * cs + core
    my_q = z * ys + yl

    def ctx_of(z_, x_, y_, c_):
        return ((z_ * xs + x_) * ys + y_) * cs + c_

    sibling = (ctx_of(z, x, yl, 1 - core), group)
    x_peers = []
    for step in range(1, xs):
        other = lax.rem(x + step, xs)
        x_peers.append((other * cs + core, (ctx_of(z, other, yl, core), group)))

    def q_peer(offset):
        block = lax.rem(my_q + offset, nq)
        return block, (ctx_of(block // ys, x, lax.rem(block, ys), core), group)

    q_peers = [q_peer(step) for step in range(1, nq)]
    partner = (me, 1 - group)
    right = (lax.rem(me + 1, count), group)
    left = (lax.rem(me + count - 1, count), group)

    barrier = pltpu.get_barrier_semaphore()
    everyone = [sibling, partner, right, left]
    everyone += [peer for _, peer in x_peers] + [peer for _, peer in q_peers]
    for peer in everyone:
        pl.semaphore_signal(barrier, inc=1, device_id=peer, device_id_type=MESH)

    plain = frames_ref[...].astype(jnp.float32)
    slope = tangent_ref[...].astype(jnp.float32)
    gain = gain_ref[...]
    inverse = lax.rsqrt(jnp.mean(plain * plain, axis=-1, keepdims=True) + EPSILON)
    cross = jnp.mean(plain * slope, axis=-1, keepdims=True)
    normed = (plain * inverse * gain).astype(jnp.bfloat16)
    normed_slope = (
        gain * (slope * inverse - plain * inverse * inverse * inverse * cross)
    ).astype(jnp.bfloat16)
    both = jnp.concatenate([normed, normed_slope], axis=0)

    def project(weight_ref):
        return jnp.dot(both, weight_ref[...], preferred_element_type=jnp.float32)

    keys = project(wk_ref)
    low = lax.broadcasted_iota(jnp.int32, (ROWS, 2 * HDIM), 1) < HDIM
    for pair in range(heads // 2):
        cols = slice(pair * 2 * HDIM, (pair + 1) * 2 * HDIM)
        key_pair, slope_pair = keys[:ROWS, cols], keys[ROWS:, cols]
        even = jnp.where(low, key_pair, pltpu.roll(slope_pair, HDIM, 1))
        odd = jnp.where(low, pltpu.roll(key_pair, HDIM, 1), slope_pair)
        kv[2 * pair, my_k, 0] = even.astype(jnp.bfloat16)
        kv[2 * pair + 1, my_k, 0] = odd.astype(jnp.bfloat16)

    def turned(values):
        return (
            values[:ROWS].T.astype(jnp.bfloat16),
            values[ROWS:].T.astype(jnp.bfloat16),
        )

    queries, query_slope = turned(project(wq_ref))
    queries, query_slope = queries * 0.125, query_slope * 0.125
    values, value_slope = turned(project(wv_ref))
    for h in range(heads):
        rows = slice(h * HDIM, (h + 1) * HDIM)
        qq[h, my_q, :HDIM] = queries[rows]
        qq[h, my_q, HDIM:] = query_slope[rows]
        kv[h, my_k, 1, :HDIM] = values[rows]
        kv[h, my_k, 1, HDIM:] = value_slope[rows]

    pl.semaphore_wait(barrier, len(everyone))

    def kv_copy(h, block, peer):
        return pltpu.make_async_remote_copy(
            src_ref=kv.at[h, block],
            dst_ref=kv.at[h, block],
            send_sem=kv_send.at[h],
            recv_sem=kv_recv.at[h, block],
            device_id=peer,
            device_id_type=MESH,
        )

    def q_copy(h, peer):
        return pltpu.make_async_remote_copy(
            src_ref=qq.at[h, my_q],
            dst_ref=qq.at[h, my_q],
            send_sem=q_send.at[h],
            recv_sem=q_recv.at[h],
            device_id=peer,
            device_id_type=MESH,
        )

    @pl.loop(0, heads)
    def _(h):
        for _, peer in x_peers:
            kv_copy(h, my_k, peer).start()
        for _, peer in q_peers:
            q_copy(h, peer).start()
        kv_copy(h, my_k, sibling).start()

    wo_copy = pltpu.make_async_remote_copy(
        src_ref=wo_ref.at[:, pl.ds(pl.multiple_of((1 - group) * half, 128), half)],
        dst_ref=wo_far,
        send_sem=wo_sem.at[0],
        recv_sem=wo_sem.at[1],
        device_id=partner,
        device_id_type=MESH,
    )
    wo_copy.start()

    def kv_arrived(h, block):
        pltpu.make_async_copy(kv.at[h, block], kv.at[h, block], kv_recv.at[h, block]).wait()

    def forward(h):
        for block, _ in x_peers:
            kv_arrived(h, block)
            kv_copy(h, block, sibling).start()

    def part_copy(h, offset):
        block, peer = q_peer(offset)
        return pltpu.make_async_remote_copy(
            src_ref=part_out.at[h, block],
            dst_ref=part_in.at[h, my_q],
            send_sem=part_send.at[h],
            recv_sem=part_recv.at[h],
            device_id=peer,
            device_id_type=MESH,
        )

    def head_copy(h):
        here = joined.at[group, h]
        return pltpu.make_async_remote_copy(
            src_ref=here,
            dst_ref=here,
            send_sem=head_send.at[h],
            recv_sem=head_recv.at[h],
            device_id=partner,
            device_id_type=MESH,
        )

    def attend(h, tile):
        first = lax.rem(my_q + 2 * tile + 1, nq)
        second = lax.rem(my_q + 2 * tile + 2, nq)
        key_rows = kv[h, :, 0].reshape(nk * ROWS, 2 * HDIM)
        value_cols = jnp.concatenate([kv[h, b, 1] for b in range(nk)], axis=1)
        near, far = qq[h, first], qq[h, second]
        plain_q = jnp.concatenate([near[:HDIM], far[:HDIM]], axis=1)
        slope_q = jnp.concatenate([near[HDIM:], far[HDIM:]], axis=1)
        top = jnp.concatenate([plain_q, slope_q], axis=1)
        bottom = jnp.concatenate([jnp.zeros_like(plain_q), plain_q], axis=1)
        product = jnp.dot(
            key_rows, jnp.concatenate([top, bottom], axis=0), preferred_element_type=jnp.float32
        )
        width = 2 * ROWS
        scores, slopes = product[:, :width], product[:, width:]
        peak = jnp.max(scores, axis=0, keepdims=True)
        weights = jnp.exp(scores - peak)
        slanted = weights * slopes
        totals = jnp.sum(weights, axis=0, keepdims=True)
        moments = jnp.sum(slanted, axis=0, keepdims=True)
        stacked = jnp.concatenate(
            [weights.astype(jnp.bfloat16), slanted.astype(jnp.bfloat16)], axis=1
        )
        sums = jnp.dot(value_cols, stacked, preferred_element_type=jnp.float32)
        share = 1.0 / totals
        center = moments * share
        attended = sums[:HDIM, :width] * share
        tilted = (sums[HDIM:, :width] + sums[:HDIM, width:]) * share - center * attended
        stats = split3(peak + jnp.log(totals)) + split3(center)
        stats = jnp.concatenate(
            [s.astype(jnp.float32) for s in stats]
            + [jnp.zeros((STAT - len(stats), width), jnp.float32)],
            axis=0,
        ).astype(jnp.bfloat16)
        attended, tilted = attended.astype(jnp.bfloat16), tilted.astype(jnp.bfloat16)
        for place, block in enumerate((first, second)):
            cols = slice(place * ROWS, (place + 1) * ROWS)
            part_out[h, block, :HDIM] = attended[:, cols]
            part_out[h, block, HDIM : 2 * HDIM] = tilted[:, cols]
            part_out[h, block, 2 * HDIM :] = stats[:, cols]

    def combine(h):
        part_in[h, my_q] = part_out[h, my_q]
        landed = part_in.at[h, pl.ds(0, nq - 1)]
        pltpu.make_async_copy(landed, landed, part_recv.at[h]).wait()
        logs, centers = [], []
        for b in range(nq):
            stats = part_in[h, b, 2 * HDIM :].astype(jnp.float32)
            logs.append(stats[0:1] + stats[1:2] + stats[2:3])
            centers.append(stats[3:4] + stats[4:5] + stats[5:6])
        top = functools.reduce(jnp.maximum, logs)
        shares = [jnp.exp(entry - top) for entry in logs]
        scale = 1.0 / functools.reduce(jnp.add, shares)
        shares = [entry * scale for entry in shares]
        middle = functools.reduce(jnp.add, [s * c for s, c in zip(shares, centers)])
        attended = jnp.zeros((HDIM, ROWS), jnp.float32)
        tilted = jnp.zeros((HDIM, ROWS), jnp.float32)
        for b in range(nq):
            piece = part_in[h, b, :HDIM].astype(jnp.float32) * shares[b]
            attended = attended + piece
            tilted = tilted + part_in[h, b, HDIM : 2 * HDIM].astype(jnp.float32) * shares[b]
            tilted = tilted + piece * (centers[b] - middle)
        joined[group, h, :HDIM] = attended.astype(jnp.bfloat16)
        joined[group, h, HDIM:] = tilted.astype(jnp.bfloat16)
        head_copy(h).start()

    forward(0)

    @pl.loop(0, heads)
    def _(h):
        for step in range(xs):
            kv_arrived(h, lax.rem(x + step, xs) * cs + 1 - core)
        landed = qq.at[h, pl.ds(0, nq - 1)]
        pltpu.make_async_copy(landed, landed, q_recv.at[h]).wait()

        @pl.loop(0, nq // 2)
        def _(tile):
            attend(h, tile)
            part_copy(h, 2 * tile + 1).start()

            @pl.when(tile < nq // 2 - 1)
            def _():
                part_copy(h, 2 * tile + 2).start()

            @pl.when(jnp.logical_and(tile == 0, h < heads - 1))
            def _():
                forward(h + 1)

        @pl.when(h >= 2)
        def _():
            combine(h - 2)

    for h in range(max(heads - 2, 0), heads):
        combine(h)

    wo_copy.wait()
    for h in range(heads):
        head_copy(h).wait()

    offset = pl.multiple_of(group * half, 128)
    own_cols = pl.ds(offset, half)

    def rows_of(source, lower):
        stacked = joined[source, :, lower : lower + HDIM].reshape(half, ROWS)
        return stacked.astype(jnp.float32).T.astype(jnp.bfloat16)

    def heads_of(source):
        return jnp.concatenate([rows_of(source, 0), rows_of(source, HDIM)], axis=0)

    mixing = jnp.dot(heads_of(group), wo_ref[:, own_cols], preferred_element_type=jnp.float32)
    mixing += jnp.dot(heads_of(1 - group), wo_far[...], preferred_element_type=jnp.float32)
    padded[0, MARGIN : MARGIN + ROWS] = (
        frames_ref[:, own_cols].astype(jnp.float32) + mixing[:ROWS]
    ).astype(jnp.bfloat16)
    padded[1, MARGIN : MARGIN + ROWS] = (
        tangent_ref[:, own_cols].astype(jnp.float32) + mixing[ROWS:]
    ).astype(jnp.bfloat16)

    to_right = pltpu.make_async_remote_copy(
        src_ref=padded.at[:, pl.ds(ROWS, MARGIN)],
        dst_ref=padded.at[:, pl.ds(0, MARGIN)],
        send_sem=halo_sem.at[0],
        recv_sem=halo_sem.at[1],
        device_id=right,
        device_id_type=MESH,
    )
    to_left = pltpu.make_async_remote_copy(
        src_ref=padded.at[:, pl.ds(MARGIN, MARGIN)],
        dst_ref=padded.at[:, pl.ds(ROWS + MARGIN, MARGIN)],
        send_sem=halo_sem.at[2],
        recv_sem=halo_sem.at[3],
        device_id=left,
        device_id_type=MESH,
    )
    to_right.start()
    to_left.start()
    to_right.wait()
    to_left.wait()
    wide[...] = padded[...].astype(jnp.float32)

    taps = taps_ref.shape[0]
    reach = MARGIN - taps // 2

    def act_copy(chunk):
        here = act.at[group, chunk]
        return pltpu.make_async_remote_copy(
            src_ref=here,
            dst_ref=here,
            send_sem=act_send.at[chunk],
            recv_sem=act_recv.at[chunk],
            device_id=partner,
            device_id_type=MESH,
        )

    chunks = half // 128
    for chunk in range(chunks):
        cols = slice(chunk * 128, (chunk + 1) * 128)
        far_cols = pl.ds(pl.multiple_of(offset + chunk * 128, 128), 128)
        weights = taps_ref[:, far_cols]
        filtered = []
        for which in range(2):
            total = jnp.zeros((ROWS, 128), jnp.float32)
            for phase in range(8):
                partial = None
                for tap in range(phase, taps, 8):
                    start = tap - phase
                    term = weights[tap : tap + 1] * wide[which, start : start + ROWS + 8, cols]
                    partial = term if partial is None else partial + term
                total = total + partial[phase + reach : phase + reach + ROWS]
            filtered.append(total)
        preact = filtered[0] + bias_ref[:, far_cols]
        gating = 1.0 / (1.0 + jnp.exp(-preact))
        act[group, chunk, 0] = (preact * gating).astype(jnp.bfloat16)
        act[group, chunk, 1] = (
            gating * (1.0 + preact * (1.0 - gating)) * filtered[1]
        ).astype(jnp.bfloat16)
        act_copy(chunk).start()

    def mix(source):
        rows = jnp.concatenate(
            [act[source, chunk].reshape(2 * ROWS, 128) for chunk in range(chunks)], axis=1
        )
        weight = wm_ref[pl.ds(pl.multiple_of(source * half, 128), half), :]
        return jnp.dot(rows, weight, preferred_element_type=jnp.float32)

    total = mix(group)
    for chunk in range(chunks):
        act_copy(chunk).wait()
    total = total + mix(1 - group)
    out_ref[...] = (wide[0, MARGIN : MARGIN + ROWS] + total[:ROWS]).astype(jnp.bfloat16)
    slope_ref[...] = (wide[1, MARGIN : MARGIN + ROWS] + total[ROWS:]).astype(jnp.bfloat16)

    @pl.loop(0, heads)
    def _(h):
        sent = kv.at[h, pl.ds(0, xs - 1 + 1 + xs - 1)]
        pltpu.make_async_copy(sent, sent, kv_send.at[h]).wait()
        sent = qq.at[h, pl.ds(0, nq - 1)]
        pltpu.make_async_copy(sent, sent, q_send.at[h]).wait()
        sent = part_out.at[h, pl.ds(0, nq - 1)]
        pltpu.make_async_copy(sent, sent, part_send.at[h]).wait()


def shards(
    sizes,
    frames,
    tangent,
    norm_gain,
    query_weight,
    key_weight,
    value_weight,
    out_weight,
    conv_weight,
    conv_bias,
    mix_weight,
):
    zs, xs, ys, cs = sizes
    nk, nq = xs * cs, zs * ys
    half = query_weight.shape[1]
    heads = half // HDIM
    sem = pltpu.SemaphoreType.DMA
    vmem = pl.BlockSpec(memory_space=pltpu.VMEM)
    shape = jax.ShapeDtypeStruct((ROWS, half), jnp.bfloat16)
    return pl.pallas_call(
        functools.partial(kernel, sizes, heads),
        out_shape=(shape, shape),
        in_specs=[vmem] * 10,
        out_specs=(vmem, vmem),
        scratch_shapes=[
            pltpu.VMEM((heads, nk, 2, ROWS, 2 * HDIM), jnp.bfloat16),
            pltpu.VMEM((heads, nq, 2 * HDIM, ROWS), jnp.bfloat16),
            pltpu.VMEM((heads, nq, 2 * HDIM + STAT, ROWS), jnp.bfloat16),
            pltpu.VMEM((heads, nq, 2 * HDIM + STAT, ROWS), jnp.bfloat16),
            pltpu.VMEM((2, heads, 2 * HDIM, ROWS), jnp.bfloat16),
            pltpu.VMEM((half, half), jnp.bfloat16),
            pltpu.VMEM((2, ROWS + 2 * MARGIN, half), jnp.bfloat16),
            pltpu.VMEM((2, ROWS + 2 * MARGIN, half), jnp.float32),
            pltpu.VMEM((2, half // 128, 2, ROWS, 128), jnp.bfloat16),
            sem((heads,)),
            sem((heads, nk)),
            sem((heads,)),
            sem((heads,)),
            sem((heads,)),
            sem((heads,)),
            sem((heads,)),
            sem((heads,)),
            sem((2,)),
            sem((4,)),
            sem((half // 128,)),
            sem((half // 128,)),
        ],
        compiler_params=pltpu.CompilerParams(
            collective_id=0, has_side_effects=True, vmem_limit_bytes=48 * 1024 * 1024
        ),
        name="block",
    )(
        frames,
        tangent,
        norm_gain.reshape(1, -1),
        query_weight,
        key_weight,
        value_weight,
        out_weight,
        conv_weight,
        conv_bias.reshape(1, -1),
        mix_weight,
    )


def solution(mesh):
    sizes = FACTORS[mesh.shape["ctx"]]
    placed = (
        P("ctx", None),
        P("ctx", None),
        P(),
        P(None, "head"),
        P(None, "head"),
        P(None, "head"),
        P("head", None),
        P(),
        P(),
        P(None, "head"),
    )
    return jax.shard_map(
        functools.partial(shards, sizes),
        mesh=mesh,
        in_specs=placed,
        out_specs=(P("ctx", "head"), P("ctx", "head")),
        check_vma=False,
    )
```

```python
import functools

import jax
import jax.numpy as jnp
from jax import lax
from jax.experimental import pallas as pl
from jax.experimental.pallas import tpu as pltpu
from jax.sharding import PartitionSpec as P

MESH = pl.DeviceIdType.MESH
HDIM = 64
EPSILON = 1e-06
ROWS = 128
STAT = 16
MARGIN = 16
FACTORS = {64: (4, 4, 2, 2)}


def split3(value):
    first = value.astype(jnp.bfloat16)
    rest = value - first.astype(jnp.float32)
    second = rest.astype(jnp.bfloat16)
    third = (rest - second.astype(jnp.float32)).astype(jnp.bfloat16)
    return [first, second, third]


def kernel(
    sizes,
    heads,
    frames_hbm,
    tangent_hbm,
    gain_hbm,
    wq_hbm,
    wk_hbm,
    wv_hbm,
    wo_hbm,
    taps_hbm,
    bias_hbm,
    wm_hbm,
    out_ref,
    slope_ref,
    frames_ref,
    tangent_ref,
    gain_ref,
    wq_ref,
    wk_ref,
    wv_ref,
    wo_ref,
    taps_ref,
    bias_ref,
    wm_ref,
    stage_kv,
    stage_q,
    kv,
    qq,
    part_out,
    part_in,
    merged,
    joined,
    wo_far,
    padded,
    wide,
    act,
    load_sem,
    relay_sem,
    relay_q_sem,
    kv_send,
    direct_recv,
    sibling_recv,
    q_send,
    q_recv,
    part_send,
    part_recv,
    head_send,
    head_recv,
    wo_sem,
    halo_sem,
    act_send,
    act_recv,
):
    zs, xs, ys, cs = sizes
    count = zs * xs * ys * cs
    half = heads * HDIM
    own = heads // ys
    nk = xs * cs * ys
    span = ys * ROWS
    me = lax.axis_index("ctx")
    group = lax.axis_index("head")
    core = lax.rem(me, cs)
    yl = lax.rem(me // cs, ys)
    x = lax.rem(me // (cs * ys), xs)
    z = me // (cs * ys * xs)

    def ctx_of(z_, x_, y_, c_):
        return ((z_ * xs + x_) * ys + y_) * cs + c_

    sibling = (ctx_of(z, x, yl, 1 - core), group)
    fellow = (ctx_of(z, x, 1 - yl, core), group)
    partner = (me, 1 - group)
    diagonal = (ctx_of(z, x, 1 - yl, core), 1 - group)
    right = (lax.rem(me + 1, count), group)
    left = (lax.rem(me + count - 1, count), group)
    x_peers = []
    for step in range(1, xs):
        other = lax.rem(x + step, xs)
        x_peers.append((other, (ctx_of(z, other, yl, core), group)))

    def z_peer(step):
        other = lax.rem(z + step, zs)
        return other, (ctx_of(other, x, yl, core), group)

    z_peers = [z_peer(step) for step in range(1, zs)]

    loads = []
    for source, target in (
        (frames_hbm, frames_ref),
        (tangent_hbm, tangent_ref),
        (gain_hbm, gain_ref),
        (wk_hbm, wk_ref),
        (wv_hbm, wv_ref),
        (wq_hbm, wq_ref),
        (wo_hbm, wo_ref),
        (wm_hbm, wm_ref),
        (taps_hbm, taps_ref),
        (bias_hbm, bias_ref),
    ):
        load = pltpu.make_async_copy(source, target, load_sem.at[len(loads)])
        load.start()
        loads.append(load)

    barrier = pltpu.get_barrier_semaphore()
    everyone = [sibling, fellow, partner, diagonal, right, left]
    everyone += [peer for _, peer in x_peers] + [peer for _, peer in z_peers]
    for peer in everyone:
        pl.semaphore_signal(barrier, inc=1, device_id=peer, device_id_type=MESH)

    def send(source, target, send_sem, recv_sem, peer):
        return pltpu.make_async_remote_copy(
            src_ref=source,
            dst_ref=target,
            send_sem=send_sem,
            recv_sem=recv_sem,
            device_id=peer,
            device_id_type=MESH,
        )

    def drain(ref, sem):
        pltpu.make_async_copy(ref, ref, sem).wait()

    for load in loads[:3]:
        load.wait()
    plain = frames_ref[...].astype(jnp.float32)
    slope = tangent_ref[...].astype(jnp.float32)
    gain = gain_ref[...]
    inverse = lax.rsqrt(jnp.mean(plain * plain, axis=-1, keepdims=True) + EPSILON)
    cross = jnp.mean(plain * slope, axis=-1, keepdims=True)
    normed = (plain * inverse * gain).astype(jnp.bfloat16)
    normed_slope = (
        gain * (slope * inverse - plain * inverse * inverse * inverse * cross)
    ).astype(jnp.bfloat16)
    both = jnp.concatenate([normed, normed_slope], axis=0)

    def project(weight_ref):
        return jnp.dot(both, weight_ref[...], preferred_element_type=jnp.float32)

    loads[3].wait()
    keys = project(wk_ref)
    low = lax.broadcasted_iota(jnp.int32, (ROWS, 2 * HDIM), 1) < HDIM
    for pair in range(heads // 2):
        cols = slice(pair * 2 * HDIM, (pair + 1) * 2 * HDIM)
        key_pair, slope_pair = keys[:ROWS, cols], keys[ROWS:, cols]
        even = jnp.where(low, key_pair, pltpu.roll(slope_pair, HDIM, 1))
        odd = jnp.where(low, pltpu.roll(key_pair, HDIM, 1), slope_pair)
        for h, value in ((2 * pair, even), (2 * pair + 1, odd)):
            stage_kv[h // own, h % own, 0] = value.astype(jnp.bfloat16)

    def turned(values):
        return (
            values[:ROWS].T.astype(jnp.bfloat16),
            values[ROWS:].T.astype(jnp.bfloat16),
        )

    loads[4].wait()
    values, value_slope = turned(project(wv_ref))
    loads[5].wait()
    queries, query_slope = turned(project(wq_ref))
    queries, query_slope = queries * 0.125, query_slope * 0.125
    for h in range(heads):
        rows = slice(h * HDIM, (h + 1) * HDIM)
        stage_kv[h // own, h % own, 1, :HDIM] = values[rows]
        stage_kv[h // own, h % own, 1, HDIM:] = value_slope[rows]
        stage_q[h // own, h % own, :HDIM] = queries[rows]
        stage_q[h // own, h % own, HDIM:] = query_slope[rows]

    pl.semaphore_wait(barrier, len(everyone))

    def slot(x_, c_, y_):
        return (x_ * cs + c_) * ys + y_

    def relay_kv(j):
        return send(
            stage_kv.at[1 - yl, j],
            kv.at[j, slot(x, core, yl)],
            relay_sem.at[0, j],
            relay_sem.at[1, j],
            fellow,
        )

    def relay_q(j):
        return send(
            stage_q.at[1 - yl, j],
            qq.at[j, z * ys + yl],
            relay_q_sem.at[0, j],
            relay_q_sem.at[1, j],
            fellow,
        )

    def direct(j, which, peer):
        here = kv.at[j, slot(x, core, which)]
        return send(here, here, kv_send.at[j], direct_recv.at[j, x, which], peer)

    def pass_on(j, source):
        here = kv.at[j, pl.ds(slot(source, core, 0), ys)]
        return send(here, here, kv_send.at[j], sibling_recv.at[j, source], sibling)

    for j in range(own):
        relay_kv(j).start()
        relay_q(j).start()
        kv[j, slot(x, core, yl)] = stage_kv[yl, j]
        qq[j, z * ys + yl] = stage_q[yl, j]
        for _, peer in x_peers:
            direct(j, yl, peer).start()

    def relay(j):
        relay_kv(j).wait()
        for _, peer in x_peers:
            direct(j, 1 - yl, peer).start()
        pass_on(j, x).start()
        relay_q(j).wait()
        here = qq.at[j, pl.ds(z * ys, ys)]
        for _, peer in z_peers:
            send(here, here, q_send.at[j], q_recv.at[j], peer).start()

    def forward(j):
        for other, _ in x_peers:
            for which in range(ys):
                drain(kv.at[j, slot(other, core, which)], direct_recv.at[j, other, which])
            pass_on(j, other).start()

    relay(0)
    relay(1)
    loads[6].wait()
    wo_copy = send(
        wo_ref.at[:, pl.ds(pl.multiple_of((1 - group) * half, 128), half)],
        wo_far,
        wo_sem.at[0],
        wo_sem.at[1],
        partner,
    )
    wo_copy.start()
    forward(0)
    for j in range(2, own):
        relay(j)

    def attend(j, other):
        key_rows = kv[j, :, 0].reshape(nk * ROWS, 2 * HDIM)
        value_cols = jnp.concatenate([kv[j, b, 1] for b in range(nk)], axis=1)
        blocks = [qq[j, other * ys + y] for y in range(ys)]
        plain_q = jnp.concatenate([block[:HDIM] for block in blocks], axis=1)
        slope_q = jnp.concatenate([block[HDIM:] for block in blocks], axis=1)
        top = jnp.concatenate([plain_q, slope_q], axis=1)
        bottom = jnp.concatenate([jnp.zeros_like(plain_q), plain_q], axis=1)
        product = jnp.dot(
            key_rows, jnp.concatenate([top, bottom], axis=0), preferred_element_type=jnp.float32
        )
        scores, slopes = product[:, :span], product[:, span:]
        peak = jnp.max(scores, axis=0, keepdims=True)
        weights = jnp.exp(scores - peak)
        slanted = weights * slopes
        totals = jnp.sum(weights, axis=0, keepdims=True)
        moments = jnp.sum(slanted, axis=0, keepdims=True)
        stacked = jnp.concatenate(
            [weights.astype(jnp.bfloat16), slanted.astype(jnp.bfloat16)], axis=1
        )
        sums = jnp.dot(value_cols, stacked, preferred_element_type=jnp.float32)
        share = 1.0 / totals
        center = moments * share
        attended = sums[:HDIM, :span] * share
        tilted = (sums[HDIM:, :span] + sums[:HDIM, span:]) * share - center * attended
        stats = split3(peak + jnp.log(totals)) + split3(center)
        stats = jnp.concatenate(
            [s.astype(jnp.float32) for s in stats]
            + [jnp.zeros((STAT - len(stats), span), jnp.float32)],
            axis=0,
        )
        part_out[j, other, :HDIM] = attended.astype(jnp.bfloat16)
        part_out[j, other, HDIM : 2 * HDIM] = tilted.astype(jnp.bfloat16)
        part_out[j, other, 2 * HDIM :] = stats.astype(jnp.bfloat16)

    def combine(j):
        part_in[j, z] = part_out[j, z]
        if zs > 1:
            drain(part_in.at[j, pl.ds(0, zs - 1)], part_recv.at[j])
        logs, centers = [], []
        for b in range(zs):
            stats = part_in[j, b, 2 * HDIM :].astype(jnp.float32)
            logs.append(stats[0:1] + stats[1:2] + stats[2:3])
            centers.append(stats[3:4] + stats[4:5] + stats[5:6])
        top = functools.reduce(jnp.maximum, logs)
        shares = [jnp.exp(entry - top) for entry in logs]
        scale = 1.0 / functools.reduce(jnp.add, shares)
        shares = [entry * scale for entry in shares]
        middle = functools.reduce(jnp.add, [s * c for s, c in zip(shares, centers)])
        attended = jnp.zeros((HDIM, span), jnp.float32)
        tilted = jnp.zeros((HDIM, span), jnp.float32)
        for b in range(zs):
            piece = part_in[j, b, :HDIM].astype(jnp.float32) * shares[b]
            attended = attended + piece
            tilted = tilted + part_in[j, b, HDIM : 2 * HDIM].astype(jnp.float32) * shares[b]
            tilted = tilted + piece * (centers[b] - middle)
        result = jnp.concatenate([attended, tilted], axis=0).astype(jnp.bfloat16)
        for y in range(ys):
            merged[j, y] = result[:, y * ROWS : (y + 1) * ROWS]
        here = joined.at[group, yl, j]
        for peer, row_block in ((fellow, 1 - yl), (diagonal, 1 - yl), (partner, yl)):
            send(merged.at[j, row_block], here, head_send.at[j], head_recv.at[j], peer).start()
        joined[group, yl, j] = merged[j, yl]

    @pl.loop(0, own)
    def _(j):
        for step in range(xs):
            source = lax.rem(x + step, xs)
            drain(
                kv.at[j, pl.ds(slot(source, 1 - core, 0), ys)], sibling_recv.at[j, source]
            )
        if zs > 1:
            drain(qq.at[j, pl.ds(0, ys * (zs - 1))], q_recv.at[j])

        @pl.loop(0, zs)
        def _(tile):
            other, peer = z_peer(tile + 1)
            attend(j, other)

            @pl.when(tile < zs - 1)
            def _():
                send(
                    part_out.at[j, other],
                    part_in.at[j, z],
                    part_send.at[j],
                    part_recv.at[j],
                    peer,
                ).start()

            @pl.when(jnp.logical_and(tile == 0, j < own - 1))
            def _():
                forward(j + 1)

        @pl.when(j >= 1)
        def _():
            combine(j - 1)

    combine(own - 1)

    wo_copy.wait()
    for j in range(own):
        drain(joined.at[0, 0, pl.ds(0, 3)], head_recv.at[j])

    offset = pl.multiple_of(group * half, 128)
    own_cols = pl.ds(offset, half)

    def rows_of(source, lower):
        stacked = joined[source, :, :, lower : lower + HDIM].reshape(half, ROWS)
        return stacked.astype(jnp.float32).T.astype(jnp.bfloat16)

    def heads_of(source):
        return jnp.concatenate([rows_of(source, 0), rows_of(source, HDIM)], axis=0)

    mixing = jnp.dot(heads_of(group), wo_ref[:, own_cols], preferred_element_type=jnp.float32)
    mixing += jnp.dot(heads_of(1 - group), wo_far[...], preferred_element_type=jnp.float32)
    padded[0, MARGIN : MARGIN + ROWS] = (
        frames_ref[:, own_cols].astype(jnp.float32) + mixing[:ROWS]
    ).astype(jnp.bfloat16)
    padded[1, MARGIN : MARGIN + ROWS] = (
        tangent_ref[:, own_cols].astype(jnp.float32) + mixing[ROWS:]
    ).astype(jnp.bfloat16)

    to_right = send(
        padded.at[:, pl.ds(ROWS, MARGIN)],
        padded.at[:, pl.ds(0, MARGIN)],
        halo_sem.at[0],
        halo_sem.at[1],
        right,
    )
    to_left = send(
        padded.at[:, pl.ds(MARGIN, MARGIN)],
        padded.at[:, pl.ds(ROWS + MARGIN, MARGIN)],
        halo_sem.at[2],
        halo_sem.at[3],
        left,
    )
    to_right.start()
    to_left.start()
    for load in loads[7:]:
        load.wait()
    to_right.wait()
    to_left.wait()
    wide[...] = padded[...].astype(jnp.float32)

    taps = taps_ref.shape[0]
    reach = MARGIN - taps // 2

    def act_copy(chunk):
        here = act.at[group, chunk]
        return send(here, here, act_send.at[chunk], act_recv.at[chunk], partner)

    chunks = half // 128
    for chunk in range(chunks):
        cols = slice(chunk * 128, (chunk + 1) * 128)
        far_cols = pl.ds(pl.multiple_of(offset + chunk * 128, 128), 128)
        weights = taps_ref[:, far_cols]
        filtered = []
        for which in range(2):
            total = jnp.zeros((ROWS, 128), jnp.float32)
            for phase in range(8):
                partial = None
                for tap in range(phase, taps, 8):
                    start = tap - phase
                    term = weights[tap : tap + 1] * wide[which, start : start + ROWS + 8, cols]
                    partial = term if partial is None else partial + term
                total = total + partial[phase + reach : phase + reach + ROWS]
            filtered.append(total)
        preact = filtered[0] + bias_ref[:, far_cols]
        gating = 1.0 / (1.0 + jnp.exp(-preact))
        act[group, chunk, 0] = (preact * gating).astype(jnp.bfloat16)
        act[group, chunk, 1] = (
            gating * (1.0 + preact * (1.0 - gating)) * filtered[1]
        ).astype(jnp.bfloat16)
        act_copy(chunk).start()

    def mix(source):
        rows = jnp.concatenate(
            [act[source, chunk].reshape(2 * ROWS, 128) for chunk in range(chunks)], axis=1
        )
        weight = wm_ref[pl.ds(pl.multiple_of(source * half, 128), half), :]
        return jnp.dot(rows, weight, preferred_element_type=jnp.float32)

    total = mix(group)
    for chunk in range(chunks):
        act_copy(chunk).wait()
    total = total + mix(1 - group)
    out_ref[...] = (wide[0, MARGIN : MARGIN + ROWS] + total[:ROWS]).astype(jnp.bfloat16)
    slope_ref[...] = (wide[1, MARGIN : MARGIN + ROWS] + total[ROWS:]).astype(jnp.bfloat16)

    for j in range(own):
        drain(kv.at[j, pl.ds(0, 2 * ys * (xs - 1) + ys)], kv_send.at[j])
        if zs > 1:
            drain(qq.at[j, pl.ds(0, ys * (zs - 1))], q_send.at[j])
            drain(part_out.at[j, pl.ds(0, zs - 1)], part_send.at[j])
        drain(joined.at[0, 0, pl.ds(0, 3)], head_send.at[j])


def shards(
    sizes,
    frames,
    tangent,
    norm_gain,
    query_weight,
    key_weight,
    value_weight,
    out_weight,
    conv_weight,
    conv_bias,
    mix_weight,
):
    zs, xs, ys, cs = sizes
    half = query_weight.shape[1]
    heads = half // HDIM
    own = heads // ys
    nk = xs * cs * ys
    sem = pltpu.SemaphoreType.DMA
    hbm = pl.BlockSpec(memory_space=pl.ANY)
    vmem = pl.BlockSpec(memory_space=pltpu.VMEM)
    shape = jax.ShapeDtypeStruct((ROWS, half), jnp.bfloat16)
    operands = (
        frames,
        tangent,
        norm_gain.reshape(1, -1),
        query_weight,
        key_weight,
        value_weight,
        out_weight,
        conv_weight,
        conv_bias.reshape(1, -1),
        mix_weight,
    )
    part = (own, zs, 2 * HDIM + STAT, ys * ROWS)
    return pl.pallas_call(
        functools.partial(kernel, sizes, heads),
        out_shape=(shape, shape),
        in_specs=[hbm] * len(operands),
        out_specs=(vmem, vmem),
        scratch_shapes=[pltpu.VMEM(value.shape, value.dtype) for value in operands]
        + [
            pltpu.VMEM((ys, own, 2, ROWS, 2 * HDIM), jnp.bfloat16),
            pltpu.VMEM((ys, own, 2 * HDIM, ROWS), jnp.bfloat16),
            pltpu.VMEM((own, nk, 2, ROWS, 2 * HDIM), jnp.bfloat16),
            pltpu.VMEM((own, zs * ys, 2 * HDIM, ROWS), jnp.bfloat16),
            pltpu.VMEM(part, jnp.bfloat16),
            pltpu.VMEM(part, jnp.bfloat16),
            pltpu.VMEM((own, ys, 2 * HDIM, ROWS), jnp.bfloat16),
            pltpu.VMEM((2, ys, own, 2 * HDIM, ROWS), jnp.bfloat16),
            pltpu.VMEM((half, half), jnp.bfloat16),
            pltpu.VMEM((2, ROWS + 2 * MARGIN, half), jnp.bfloat16),
            pltpu.VMEM((2, ROWS + 2 * MARGIN, half), jnp.float32),
            pltpu.VMEM((2, half // 128, 2, ROWS, 128), jnp.bfloat16),
            sem((len(operands),)),
            sem((2, own)),
            sem((2, own)),
            sem((own,)),
            sem((own, xs, ys)),
            sem((own, xs)),
            sem((own,)),
            sem((own,)),
            sem((own,)),
            sem((own,)),
            sem((own,)),
            sem((own,)),
            sem((2,)),
            sem((4,)),
            sem((half // 128,)),
            sem((half // 128,)),
        ],
        compiler_params=pltpu.CompilerParams(
            collective_id=0, has_side_effects=True, vmem_limit_bytes=48 * 1024 * 1024
        ),
        name="block",
    )(*operands)


def solution(mesh):
    sizes = FACTORS[mesh.shape["ctx"]]
    placed = (
        P("ctx", None),
        P("ctx", None),
        P(),
        P(None, "head"),
        P(None, "head"),
        P(None, "head"),
        P("head", None),
        P(),
        P(),
        P(None, "head"),
    )
    return jax.shard_map(
        functools.partial(shards, sizes),
        mesh=mesh,
        in_specs=placed,
        out_specs=(P("ctx", "head"), P("ctx", "head")),
        check_vma=False,
    )
```

```python
import functools

import jax
import jax.numpy as jnp
from jax import lax
from jax.experimental import pallas as pl
from jax.experimental.pallas import tpu as pltpu
from jax.sharding import PartitionSpec as P

MESH = pl.DeviceIdType.MESH
HDIM = 64
EPSILON = 1e-06
ROWS = 128
STAT = 16
MARGIN = 16
FACTORS = {64: (4, 4, 2, 2)}


def split3(value):
    first = value.astype(jnp.bfloat16)
    rest = value - first.astype(jnp.float32)
    second = rest.astype(jnp.bfloat16)
    third = (rest - second.astype(jnp.float32)).astype(jnp.bfloat16)
    return [first, second, third]


def kernel(
    sizes,
    heads,
    frames_hbm,
    tangent_hbm,
    gain_hbm,
    wq_hbm,
    wk_hbm,
    wv_hbm,
    wo_hbm,
    taps_hbm,
    bias_hbm,
    wm_hbm,
    out_ref,
    slope_ref,
    inputs,
    gain_ref,
    wq_ref,
    wk_ref,
    wv_ref,
    wo_all,
    taps_ref,
    bias_ref,
    wm_ref,
    stage_kv,
    stage_q,
    kv,
    qq,
    part_out,
    part_in,
    merged,
    joined,
    wide,
    act,
    load_sem,
    relay_sem,
    relay_q_sem,
    kv_send,
    direct_recv,
    sibling_recv,
    q_send,
    q_recv,
    part_send,
    part_recv,
    head_send,
    head_recv,
    wo_sem,
    halo_sem,
):
    zs, xs, ys, cs = sizes
    count = zs * xs * ys * cs
    half = heads * HDIM
    own = heads // ys
    nk = xs * cs * ys
    span = ys * ROWS
    me = lax.axis_index("ctx")
    group = lax.axis_index("head")
    core = lax.rem(me, cs)
    yl = lax.rem(me // cs, ys)
    x = lax.rem(me // (cs * ys), xs)
    z = me // (cs * ys * xs)

    def ctx_of(z_, x_, y_, c_):
        return ((z_ * xs + x_) * ys + y_) * cs + c_

    sibling = (ctx_of(z, x, yl, 1 - core), group)
    fellow = (ctx_of(z, x, 1 - yl, core), group)
    partner = (me, 1 - group)
    diagonal = (ctx_of(z, x, 1 - yl, core), 1 - group)

    def after(ctx):
        return lax.rem(ctx + 1, count)

    def before(ctx):
        return lax.rem(ctx + count - 1, count)

    right, left = (after(me), group), (before(me), group)
    x_peers = []
    for step in range(1, xs):
        other = lax.rem(x + step, xs)
        x_peers.append((other, (ctx_of(z, other, yl, core), group)))

    def z_peer(step):
        other = lax.rem(z + step, zs)
        return other, (ctx_of(other, x, yl, core), group)

    z_peers = [z_peer(step) for step in range(1, zs)]

    loads = []
    body = pl.ds(MARGIN, ROWS)
    for source, target in (
        (frames_hbm, inputs.at[0, body]),
        (tangent_hbm, inputs.at[1, body]),
        (gain_hbm, gain_ref),
        (wk_hbm, wk_ref),
        (wv_hbm, wv_ref),
        (wq_hbm, wq_ref),
        (wo_hbm, wo_all.at[group]),
        (wm_hbm, wm_ref),
        (taps_hbm, taps_ref),
        (bias_hbm, bias_ref),
    ):
        load = pltpu.make_async_copy(source, target, load_sem.at[len(loads)])
        load.start()
        loads.append(load)

    barrier = pltpu.get_barrier_semaphore()
    everyone = []
    near_square = lax.rem(z * xs + x + zs * xs + 2 * core - 1, zs * xs)
    for g in (group, 1 - group):
        for y in (yl, 1 - yl):
            everyone += [(ctx_of(z, x, y, core), g), (ctx_of(z, x, y, 1 - core), g)]
            everyone.append(((near_square * ys + y) * cs + 1 - core, g))
    everyone = everyone[1:]
    everyone += [peer for _, peer in x_peers] + [peer for _, peer in z_peers]
    for peer in everyone:
        pl.semaphore_signal(barrier, inc=1, device_id=peer, device_id_type=MESH)

    def send(source, target, send_sem, recv_sem, peer):
        return pltpu.make_async_remote_copy(
            src_ref=source,
            dst_ref=target,
            send_sem=send_sem,
            recv_sem=recv_sem,
            device_id=peer,
            device_id_type=MESH,
        )

    def drain(ref, sem):
        pltpu.make_async_copy(ref, ref, sem).wait()

    for load in loads[:3]:
        load.wait()
    plain = inputs[0, body].astype(jnp.float32)
    slope = inputs[1, body].astype(jnp.float32)
    gain = gain_ref[...]
    inverse = lax.rsqrt(jnp.mean(plain * plain, axis=-1, keepdims=True) + EPSILON)
    cross = jnp.mean(plain * slope, axis=-1, keepdims=True)
    normed = (plain * inverse * gain).astype(jnp.bfloat16)
    normed_slope = (
        gain * (slope * inverse - plain * inverse * inverse * inverse * cross)
    ).astype(jnp.bfloat16)
    both = jnp.concatenate([normed, normed_slope], axis=0)

    def project(weight_ref):
        return jnp.dot(both, weight_ref[...], preferred_element_type=jnp.float32)

    loads[3].wait()
    keys = project(wk_ref)
    low = lax.broadcasted_iota(jnp.int32, (ROWS, 2 * HDIM), 1) < HDIM
    for pair in range(heads // 2):
        cols = slice(pair * 2 * HDIM, (pair + 1) * 2 * HDIM)
        key_pair, slope_pair = keys[:ROWS, cols], keys[ROWS:, cols]
        even = jnp.where(low, key_pair, pltpu.roll(slope_pair, HDIM, 1))
        odd = jnp.where(low, pltpu.roll(key_pair, HDIM, 1), slope_pair)
        for h, value in ((2 * pair, even), (2 * pair + 1, odd)):
            stage_kv[h // own, h % own, 0] = value.astype(jnp.bfloat16)

    def turned(values):
        return (
            values[:ROWS].T.astype(jnp.bfloat16),
            values[ROWS:].T.astype(jnp.bfloat16),
        )

    loads[4].wait()
    values, value_slope = turned(project(wv_ref))
    loads[5].wait()
    queries, query_slope = turned(project(wq_ref))
    queries, query_slope = queries * 0.125, query_slope * 0.125
    for h in range(heads):
        rows = slice(h * HDIM, (h + 1) * HDIM)
        stage_kv[h // own, h % own, 1, :HDIM] = values[rows]
        stage_kv[h // own, h % own, 1, HDIM:] = value_slope[rows]
        stage_q[h // own, h % own, :HDIM] = queries[rows]
        stage_q[h // own, h % own, HDIM:] = query_slope[rows]

    pl.semaphore_wait(barrier, len(everyone))

    def slot(x_, c_, y_):
        return (x_ * cs + c_) * ys + y_

    def relay_kv(j):
        return send(
            stage_kv.at[1 - yl, j],
            kv.at[j, slot(x, core, yl)],
            relay_sem.at[0, j],
            relay_sem.at[1, j],
            fellow,
        )

    def relay_q(j):
        return send(
            stage_q.at[1 - yl, j],
            qq.at[j, z * ys + yl],
            relay_q_sem.at[0, j],
            relay_q_sem.at[1, j],
            fellow,
        )

    def direct(j, which, peer):
        here = kv.at[j, slot(x, core, which)]
        return send(here, here, kv_send.at[j], direct_recv.at[j, x, which], peer)

    def pass_on(j, source):
        here = kv.at[j, pl.ds(slot(source, core, 0), ys)]
        return send(here, here, kv_send.at[j], sibling_recv.at[j, source], sibling)

    for j in range(own):
        relay_kv(j).start()
        relay_q(j).start()
        kv[j, slot(x, core, yl)] = stage_kv[yl, j]
        qq[j, z * ys + yl] = stage_q[yl, j]
        for _, peer in x_peers:
            direct(j, yl, peer).start()

    def relay(j):
        relay_kv(j).wait()
        for _, peer in x_peers:
            direct(j, 1 - yl, peer).start()
        pass_on(j, x).start()
        relay_q(j).wait()
        here = qq.at[j, pl.ds(z * ys, ys)]
        for _, peer in z_peers:
            send(here, here, q_send.at[j], q_recv.at[j], peer).start()

    def forward(j):
        for other, _ in x_peers:
            for which in range(ys):
                drain(kv.at[j, slot(other, core, which)], direct_recv.at[j, other, which])
            pass_on(j, other).start()

    relay(0)
    relay(1)
    loads[6].wait()
    here = wo_all.at[group]
    wo_copy = send(here, here, wo_sem.at[0], wo_sem.at[1], partner)
    wo_copy.start()
    to_right = send(
        inputs.at[:, pl.ds(ROWS, MARGIN)],
        inputs.at[:, pl.ds(0, MARGIN)],
        halo_sem.at[0],
        halo_sem.at[1],
        right,
    )
    to_left = send(
        inputs.at[:, pl.ds(MARGIN, MARGIN)],
        inputs.at[:, pl.ds(ROWS + MARGIN, MARGIN)],
        halo_sem.at[2],
        halo_sem.at[3],
        left,
    )
    to_right.start()
    to_left.start()
    forward(0)
    for j in range(2, own):
        relay(j)

    def attend(j, other):
        key_rows = kv[j, :, 0].reshape(nk * ROWS, 2 * HDIM)
        value_cols = jnp.concatenate([kv[j, b, 1] for b in range(nk)], axis=1)
        blocks = [qq[j, other * ys + y] for y in range(ys)]
        plain_q = jnp.concatenate([block[:HDIM] for block in blocks], axis=1)
        slope_q = jnp.concatenate([block[HDIM:] for block in blocks], axis=1)
        top = jnp.concatenate([plain_q, slope_q], axis=1)
        bottom = jnp.concatenate([jnp.zeros_like(plain_q), plain_q], axis=1)
        product = jnp.dot(
            key_rows, jnp.concatenate([top, bottom], axis=0), preferred_element_type=jnp.float32
        )
        scores, slopes = product[:, :span], product[:, span:]
        peak = jnp.max(scores, axis=0, keepdims=True)
        weights = jnp.exp(scores - peak)
        slanted = weights * slopes
        totals = jnp.sum(weights, axis=0, keepdims=True)
        moments = jnp.sum(slanted, axis=0, keepdims=True)
        stacked = jnp.concatenate(
            [weights.astype(jnp.bfloat16), slanted.astype(jnp.bfloat16)], axis=1
        )
        sums = jnp.dot(value_cols, stacked, preferred_element_type=jnp.float32)
        share = 1.0 / totals
        center = moments * share
        attended = sums[:HDIM, :span] * share
        tilted = (sums[HDIM:, :span] + sums[:HDIM, span:]) * share - center * attended
        stats = split3(peak + jnp.log(totals)) + split3(center)
        stats = jnp.concatenate(
            [s.astype(jnp.float32) for s in stats]
            + [jnp.zeros((STAT - len(stats), span), jnp.float32)],
            axis=0,
        )
        part_out[j, other, :HDIM] = attended.astype(jnp.bfloat16)
        part_out[j, other, HDIM : 2 * HDIM] = tilted.astype(jnp.bfloat16)
        part_out[j, other, 2 * HDIM :] = stats.astype(jnp.bfloat16)

    def combine(j):
        part_in[j, z] = part_out[j, z]
        if zs > 1:
            drain(part_in.at[j, pl.ds(0, zs - 1)], part_recv.at[j])
        logs, centers = [], []
        for b in range(zs):
            stats = part_in[j, b, 2 * HDIM :].astype(jnp.float32)
            logs.append(stats[0:1] + stats[1:2] + stats[2:3])
            centers.append(stats[3:4] + stats[4:5] + stats[5:6])
        top = functools.reduce(jnp.maximum, logs)
        shares = [jnp.exp(entry - top) for entry in logs]
        scale = 1.0 / functools.reduce(jnp.add, shares)
        shares = [entry * scale for entry in shares]
        middle = functools.reduce(jnp.add, [s * c for s, c in zip(shares, centers)])
        attended = jnp.zeros((HDIM, span), jnp.float32)
        tilted = jnp.zeros((HDIM, span), jnp.float32)
        for b in range(zs):
            piece = part_in[j, b, :HDIM].astype(jnp.float32) * shares[b]
            attended = attended + piece
            tilted = tilted + part_in[j, b, HDIM : 2 * HDIM].astype(jnp.float32) * shares[b]
            tilted = tilted + piece * (centers[b] - middle)
        result = jnp.concatenate([attended, tilted], axis=0)
        for y in range(ys):
            merged[j, y] = result[:, y * ROWS : (y + 1) * ROWS].T.astype(jnp.bfloat16)
        joined[group, yl, j, body] = merged[j, yl]

        def hand(source, target, peer):
            send(source, target, head_send.at[j], head_recv.at[j], peer).start()

        for peer, block in ((fellow, 1 - yl), (diagonal, 1 - yl), (partner, yl)):
            hand(merged.at[j, block], joined.at[group, yl, j, body], peer)
        for y in range(ys):
            ctx = ctx_of(z, x, y, core)
            for g in (group, 1 - group):
                hand(
                    merged.at[j, y, pl.ds(0, MARGIN)],
                    joined.at[group, yl, j, pl.ds(MARGIN + ROWS, MARGIN)],
                    (before(ctx), g),
                )
                hand(
                    merged.at[j, y, pl.ds(ROWS - MARGIN, MARGIN)],
                    joined.at[group, yl, j, pl.ds(0, MARGIN)],
                    (after(ctx), g),
                )

    @pl.loop(0, own)
    def _(j):
        for step in range(xs):
            source = lax.rem(x + step, xs)
            drain(
                kv.at[j, pl.ds(slot(source, 1 - core, 0), ys)], sibling_recv.at[j, source]
            )
        if zs > 1:
            drain(qq.at[j, pl.ds(0, ys * (zs - 1))], q_recv.at[j])

        @pl.loop(0, zs)
        def _(tile):
            other, peer = z_peer(tile + 1)
            attend(j, other)

            @pl.when(tile < zs - 1)
            def _():
                send(
                    part_out.at[j, other],
                    part_in.at[j, z],
                    part_send.at[j],
                    part_recv.at[j],
                    peer,
                ).start()

            @pl.when(jnp.logical_and(tile == 0, j < own - 1))
            def _():
                forward(j + 1)

        @pl.when(j >= 1)
        def _():
            combine(j - 1)

    combine(own - 1)

    low = lax.broadcasted_iota(jnp.int32, (ROWS + 2 * MARGIN, 2 * HDIM), 1) < HDIM

    def project_out(j):
        drain(merged.at[pl.ds(0, 2)], head_recv.at[j])
        outs, slopes, weights = [], [], []
        for g in range(2):
            first = joined[g, 0, j].astype(jnp.float32)
            second = joined[g, 1, j].astype(jnp.float32)
            outs.append(jnp.where(low, first, pltpu.roll(second, HDIM, 1)))
            slopes.append(jnp.where(low, pltpu.roll(first, HDIM, 1), second))
            for y in range(ys):
                weights.append(wo_all[g, pl.ds((y * own + j) * HDIM, HDIM)])
        rows = jnp.concatenate(
            [jnp.concatenate(outs, axis=1), jnp.concatenate(slopes, axis=1)], axis=0
        )
        return jnp.dot(
            rows.astype(jnp.bfloat16),
            jnp.concatenate(weights, axis=0),
            preferred_element_type=jnp.float32,
        )

    wo_copy.wait()
    to_right.wait()
    to_left.wait()
    mixing = functools.reduce(jnp.add, [project_out(j) for j in range(own)])
    length = ROWS + 2 * MARGIN
    for which in range(2):
        mixed = inputs[which].astype(jnp.float32) + mixing[which * length : (which + 1) * length]
        wide[which] = mixed.astype(jnp.bfloat16).astype(jnp.float32)

    for load in loads[7:]:
        load.wait()
    taps = taps_ref.shape[0]
    reach = MARGIN - taps // 2
    for chunk in range(wide.shape[2] // 128):
        cols = slice(chunk * 128, (chunk + 1) * 128)
        weights = taps_ref[:, cols]
        filtered = []
        for which in range(2):
            total = jnp.zeros((ROWS, 128), jnp.float32)
            for phase in range(8):
                partial = None
                for tap in range(phase, taps, 8):
                    start = tap - phase
                    term = weights[tap : tap + 1] * wide[which, start : start + ROWS + 8, cols]
                    partial = term if partial is None else partial + term
                total = total + partial[phase + reach : phase + reach + ROWS]
            filtered.append(total)
        preact = filtered[0] + bias_ref[:, cols]
        gating = 1.0 / (1.0 + jnp.exp(-preact))
        act[:ROWS, cols] = (preact * gating).astype(jnp.bfloat16)
        act[ROWS:, cols] = (
            gating * (1.0 + preact * (1.0 - gating)) * filtered[1]
        ).astype(jnp.bfloat16)

    total = jnp.dot(act[...], wm_ref[...], preferred_element_type=jnp.float32)
    own_cols = pl.ds(pl.multiple_of(group * half, 128), half)
    out_ref[...] = (wide[0, body, own_cols] + total[:ROWS]).astype(jnp.bfloat16)
    slope_ref[...] = (wide[1, body, own_cols] + total[ROWS:]).astype(jnp.bfloat16)

    for j in range(own):
        drain(kv.at[j, pl.ds(0, 2 * ys * (xs - 1) + ys)], kv_send.at[j])
        if zs > 1:
            drain(qq.at[j, pl.ds(0, ys * (zs - 1))], q_send.at[j])
            drain(part_out.at[j, pl.ds(0, zs - 1)], part_send.at[j])
        drain(merged.at[pl.ds(0, 2)], head_send.at[j])


def shards(
    sizes,
    frames,
    tangent,
    norm_gain,
    query_weight,
    key_weight,
    value_weight,
    out_weight,
    conv_weight,
    conv_bias,
    mix_weight,
):
    zs, xs, ys, cs = sizes
    width, half = query_weight.shape
    heads = half // HDIM
    own = heads // ys
    nk = xs * cs * ys
    length = ROWS + 2 * MARGIN
    sem = pltpu.SemaphoreType.DMA
    hbm = pl.BlockSpec(memory_space=pl.ANY)
    vmem = pl.BlockSpec(memory_space=pltpu.VMEM)
    shape = jax.ShapeDtypeStruct((ROWS, half), jnp.bfloat16)
    operands = (
        frames,
        tangent,
        norm_gain.reshape(1, -1),
        query_weight,
        key_weight,
        value_weight,
        out_weight,
        conv_weight,
        conv_bias.reshape(1, -1),
        mix_weight,
    )
    part = (own, zs, 2 * HDIM + STAT, ys * ROWS)
    return pl.pallas_call(
        functools.partial(kernel, sizes, heads),
        out_shape=(shape, shape),
        in_specs=[hbm] * len(operands),
        out_specs=(vmem, vmem),
        scratch_shapes=[
            pltpu.VMEM((2, length, width), jnp.bfloat16),
            pltpu.VMEM((1, width), jnp.float32),
            pltpu.VMEM((width, half), jnp.bfloat16),
            pltpu.VMEM((width, half), jnp.bfloat16),
            pltpu.VMEM((width, half), jnp.bfloat16),
            pltpu.VMEM((2, half, width), jnp.bfloat16),
            pltpu.VMEM(conv_weight.shape, jnp.float32),
            pltpu.VMEM((1, width), jnp.float32),
            pltpu.VMEM((width, half), jnp.bfloat16),
            pltpu.VMEM((ys, own, 2, ROWS, 2 * HDIM), jnp.bfloat16),
            pltpu.VMEM((ys, own, 2 * HDIM, ROWS), jnp.bfloat16),
            pltpu.VMEM((own, nk, 2, ROWS, 2 * HDIM), jnp.bfloat16),
            pltpu.VMEM((own, zs * ys, 2 * HDIM, ROWS), jnp.bfloat16),
            pltpu.VMEM(part, jnp.bfloat16),
            pltpu.VMEM(part, jnp.bfloat16),
            pltpu.VMEM((own, ys, ROWS, 2 * HDIM), jnp.bfloat16),
            pltpu.VMEM((2, ys, own, length, 2 * HDIM), jnp.bfloat16),
            pltpu.VMEM((2, length, width), jnp.float32),
            pltpu.VMEM((2 * ROWS, width), jnp.bfloat16),
            sem((len(operands),)),
            sem((2, own)),
            sem((2, own)),
            sem((own,)),
            sem((own, xs, ys)),
            sem((own, xs)),
            sem((own,)),
            sem((own,)),
            sem((own,)),
            sem((own,)),
            sem((own,)),
            sem((own,)),
            sem((2,)),
            sem((4,)),
        ],
        compiler_params=pltpu.CompilerParams(
            collective_id=0, has_side_effects=True, vmem_limit_bytes=60 * 1024 * 1024
        ),
        name="block",
    )(*operands)


def solution(mesh):
    sizes = FACTORS[mesh.shape["ctx"]]
    placed = (
        P("ctx", None),
        P("ctx", None),
        P(),
        P(None, "head"),
        P(None, "head"),
        P(None, "head"),
        P("head", None),
        P(),
        P(),
        P(None, "head"),
    )
    return jax.shard_map(
        functools.partial(shards, sizes),
        mesh=mesh,
        in_specs=placed,
        out_specs=(P("ctx", "head"), P("ctx", "head")),
        check_vma=False,
    )
```

```python
import functools

import jax
import jax.numpy as jnp
from jax import lax
from jax.experimental import pallas as pl
from jax.experimental.pallas import tpu as pltpu
from jax.sharding import PartitionSpec as P

MESH = pl.DeviceIdType.MESH
HDIM = 64
EPSILON = 1e-06
ROWS = 128
STAT = 16
MARGIN = 16
FACTORS = {64: (4, 4, 2, 2)}


def split3(value):
    first = value.astype(jnp.bfloat16)
    rest = value - first.astype(jnp.float32)
    second = rest.astype(jnp.bfloat16)
    third = (rest - second.astype(jnp.float32)).astype(jnp.bfloat16)
    return [first, second, third]


def kernel(
    sizes,
    heads,
    frames_hbm,
    tangent_hbm,
    gain_hbm,
    wq_hbm,
    wk_hbm,
    wv_hbm,
    wo_hbm,
    taps_hbm,
    bias_hbm,
    wm_hbm,
    out_ref,
    slope_ref,
    inputs,
    gain_ref,
    wq_ref,
    wk_ref,
    wv_ref,
    wo_all,
    taps_ref,
    bias_ref,
    wm_ref,
    stage_kv,
    stage_q,
    kv,
    qq,
    part_out,
    part_in,
    merged,
    joined,
    wide,
    act,
    product_even,
    product_odd,
    chances,
    peak_even,
    peak_odd,
    load_sem,
    relay_sem,
    relay_q_sem,
    kv_send,
    direct_recv,
    sibling_recv,
    q_send,
    q_recv,
    part_send,
    part_recv,
    head_send,
    head_recv,
    wo_sem,
    halo_sem,
):
    zs, xs, ys, cs = sizes
    count = zs * xs * ys * cs
    half = heads * HDIM
    own = heads // ys
    nk = xs * cs * ys
    span = ys * ROWS
    me = lax.axis_index("ctx")
    group = lax.axis_index("head")
    core = lax.rem(me, cs)
    yl = lax.rem(me // cs, ys)
    x = lax.rem(me // (cs * ys), xs)
    z = me // (cs * ys * xs)

    def ctx_of(z_, x_, y_, c_):
        return ((z_ * xs + x_) * ys + y_) * cs + c_

    sibling = (ctx_of(z, x, yl, 1 - core), group)
    fellow = (ctx_of(z, x, 1 - yl, core), group)
    partner = (me, 1 - group)
    diagonal = (ctx_of(z, x, 1 - yl, core), 1 - group)

    def after(ctx):
        return lax.rem(ctx + 1, count)

    def before(ctx):
        return lax.rem(ctx + count - 1, count)

    right, left = (after(me), group), (before(me), group)
    x_peers = []
    for step in sorted(range(1, xs), key=lambda step: min(step, xs - step)):
        other = lax.rem(x + step, xs)
        x_peers.append((other, (ctx_of(z, other, yl, core), group)))

    def z_peer(step):
        other = lax.rem(z + step, zs)
        return other, (ctx_of(other, x, yl, core), group)

    z_peers = [z_peer(step) for step in range(1, zs)]

    loads = []
    body = pl.ds(MARGIN, ROWS)
    for source, target in (
        (frames_hbm, inputs.at[0, body]),
        (tangent_hbm, inputs.at[1, body]),
        (gain_hbm, gain_ref),
        (wk_hbm, wk_ref),
        (wv_hbm, wv_ref),
        (wq_hbm, wq_ref),
        (wo_hbm, wo_all.at[group]),
        (wm_hbm, wm_ref),
        (taps_hbm, taps_ref),
        (bias_hbm, bias_ref),
    ):
        load = pltpu.make_async_copy(source, target, load_sem.at[len(loads)])
        load.start()
        loads.append(load)

    barrier = pltpu.get_barrier_semaphore()
    everyone = []
    near_square = lax.rem(z * xs + x + zs * xs + 2 * core - 1, zs * xs)
    for g in (group, 1 - group):
        for y in (yl, 1 - yl):
            everyone += [(ctx_of(z, x, y, core), g), (ctx_of(z, x, y, 1 - core), g)]
            everyone.append(((near_square * ys + y) * cs + 1 - core, g))
    everyone = everyone[1:]
    everyone += [peer for _, peer in x_peers] + [peer for _, peer in z_peers]
    for peer in everyone:
        pl.semaphore_signal(barrier, inc=1, device_id=peer, device_id_type=MESH)

    def send(source, target, send_sem, recv_sem, peer):
        return pltpu.make_async_remote_copy(
            src_ref=source,
            dst_ref=target,
            send_sem=send_sem,
            recv_sem=recv_sem,
            device_id=peer,
            device_id_type=MESH,
        )

    def drain(ref, sem):
        pltpu.make_async_copy(ref, ref, sem).wait()

    for load in loads[:3]:
        load.wait()
    plain = inputs[0, body].astype(jnp.float32)
    slope = inputs[1, body].astype(jnp.float32)
    gain = gain_ref[...].reshape(1, -1)
    inverse = lax.rsqrt(jnp.mean(plain * plain, axis=-1, keepdims=True) + EPSILON)
    cross = jnp.mean(plain * slope, axis=-1, keepdims=True)
    normed = (plain * inverse * gain).astype(jnp.bfloat16)
    normed_slope = (
        gain * (slope * inverse - plain * inverse * inverse * inverse * cross)
    ).astype(jnp.bfloat16)
    both = jnp.concatenate([normed, normed_slope], axis=0)

    def project(weight_ref):
        return jnp.dot(both, weight_ref[...], preferred_element_type=jnp.float32)

    loads[3].wait()
    keys = project(wk_ref)
    low = lax.broadcasted_iota(jnp.int32, (ROWS, 2 * HDIM), 1) < HDIM
    for pair in range(heads // 2):
        cols = slice(pair * 2 * HDIM, (pair + 1) * 2 * HDIM)
        key_pair, slope_pair = keys[:ROWS, cols], keys[ROWS:, cols]
        even = jnp.where(low, key_pair, pltpu.roll(slope_pair, HDIM, 1))
        odd = jnp.where(low, pltpu.roll(key_pair, HDIM, 1), slope_pair)
        for h, value in ((2 * pair, even), (2 * pair + 1, odd)):
            stage_kv[h // own, h % own, 0] = value.astype(jnp.bfloat16)

    def turned(values):
        return (
            values[:ROWS].T.astype(jnp.bfloat16),
            values[ROWS:].T.astype(jnp.bfloat16),
        )

    loads[4].wait()
    values, value_slope = turned(project(wv_ref))
    loads[5].wait()
    queries, query_slope = turned(project(wq_ref))
    queries, query_slope = queries * 0.125, query_slope * 0.125
    for h in range(heads):
        rows = slice(h * HDIM, (h + 1) * HDIM)
        stage_kv[h // own, h % own, 1, :HDIM] = values[rows]
        stage_kv[h // own, h % own, 1, HDIM:] = value_slope[rows]
        stage_q[h // own, h % own, :HDIM] = queries[rows]
        stage_q[h // own, h % own, HDIM:] = query_slope[rows]

    pl.semaphore_wait(barrier, len(everyone))

    def slot(x_, c_, y_):
        return (x_ * cs + c_) * ys + y_

    def relay_kv(j):
        return send(
            stage_kv.at[1 - yl, j],
            kv.at[j, slot(x, core, yl)],
            relay_sem.at[0, j],
            relay_sem.at[1, j],
            fellow,
        )

    def relay_q(j):
        return send(
            stage_q.at[1 - yl, j],
            qq.at[j, z * ys + yl],
            relay_q_sem.at[0, j],
            relay_q_sem.at[1, j],
            fellow,
        )

    def direct(j, which, peer):
        here = kv.at[j, slot(x, core, which)]
        return send(here, here, kv_send.at[j], direct_recv.at[j, x, which], peer)

    def pass_on(j, source):
        here = kv.at[j, pl.ds(slot(source, core, 0), ys)]
        return send(here, here, kv_send.at[j], sibling_recv.at[j, source], sibling)

    def spread(j, which):
        for _, peer in x_peers:
            direct(j, which, peer).start()

    def hand_over(j):
        relay_kv(j).start()
        relay_q(j).start()

    hand_over(0)
    for j in range(own):
        kv[j, slot(x, core, yl)] = stage_kv[yl, j]
        qq[j, z * ys + yl] = stage_q[yl, j]
        if j == 0:
            spread(0, yl)
            for other in range(1, own):
                hand_over(other)

    def relay(j):
        relay_kv(j).wait()
        spread(j, 1 - yl)
        pass_on(j, x).start()
        relay_q(j).wait()
        here = qq.at[j, pl.ds(z * ys, ys)]
        for _, peer in z_peers:
            send(here, here, q_send.at[j], q_recv.at[j, z], peer).start()
        if j < own - 1:
            spread(j + 1, yl)

    def forward(j):
        for other, _ in x_peers:
            for which in range(ys):
                drain(kv.at[j, slot(other, core, which)], direct_recv.at[j, other, which])
            pass_on(j, other).start()

    for j in range(own):
        relay(j)
    forward(0)
    loads[6].wait()
    here = wo_all.at[group]
    wo_copy = send(here, here, wo_sem.at[0], wo_sem.at[1], partner)
    wo_copy.start()
    to_right = send(
        inputs.at[:, pl.ds(ROWS, MARGIN)],
        inputs.at[:, pl.ds(0, MARGIN)],
        halo_sem.at[0],
        halo_sem.at[1],
        right,
    )
    to_left = send(
        inputs.at[:, pl.ds(MARGIN, MARGIN)],
        inputs.at[:, pl.ds(ROWS + MARGIN, MARGIN)],
        halo_sem.at[2],
        halo_sem.at[3],
        left,
    )
    to_right.start()
    to_left.start()

    tiles = own * zs
    chunk_rows = min(512, nk * ROWS)
    chunk_blocks = chunk_rows // ROWS
    step_rows = 64

    away = own * (zs - 1)

    def tile_of(u):
        if zs == 1:
            return u, 0
        early = u < away
        j = jnp.where(early, u // (zs - 1), u - away)
        return j, jnp.where(early, lax.rem(u, zs - 1), zs - 1)

    def queries_of(u):
        j, tile = tile_of(u)
        other, _ = z_peer(tile + 1)
        blocks = [qq[j, other * ys + y] for y in range(ys)]
        plain_q = jnp.concatenate([block[:HDIM] for block in blocks], axis=1)
        slope_q = jnp.concatenate([block[HDIM:] for block in blocks], axis=1)
        top = jnp.concatenate([plain_q, slope_q], axis=1)
        bottom = jnp.concatenate([jnp.zeros_like(plain_q), plain_q], axis=1)
        return jnp.concatenate([top, bottom], axis=0)

    def work(current, following, product_now, peak_now, product_next, peak_next):
        if current is not None:
            j, tile = tile_of(current)
            peak = jnp.max(peak_now[...], axis=0, keepdims=True)
            totals = jnp.zeros((8, span), jnp.float32)
            moments = jnp.zeros((8, span), jnp.float32)
            sums = None
        if following is not None:
            next_j, _ = tile_of(following)
            next_queries = queries_of(following)
            highest = jnp.full((8, span), -jnp.inf, jnp.float32)
        for first in range(0, nk, chunk_blocks):
            chunk = slice(first * ROWS, (first + chunk_blocks) * ROWS)
            if current is not None:
                for start in range(chunk.start, chunk.stop, step_rows):
                    rows = slice(start, start + step_rows)
                    weights = jnp.exp(product_now[rows, :span] - peak)
                    slanted = weights * product_now[rows, span:]
                    totals = totals + jnp.sum(weights.reshape(-1, 8, span), axis=0)
                    moments = moments + jnp.sum(slanted.reshape(-1, 8, span), axis=0)
                    chances[rows, :span] = weights.astype(jnp.bfloat16)
                    chances[rows, span:] = slanted.astype(jnp.bfloat16)
                value_cols = jnp.concatenate(
                    [kv[j, first + b, 1] for b in range(chunk_blocks)], axis=1
                )
                part = jnp.dot(value_cols, chances[chunk], preferred_element_type=jnp.float32)
                sums = part if sums is None else sums + part
            if following is not None:
                key_rows = kv[next_j, pl.ds(first, chunk_blocks), 0].reshape(chunk_rows, 2 * HDIM)
                product = jnp.dot(key_rows, next_queries, preferred_element_type=jnp.float32)
                product_next[chunk] = product
                highest = jnp.maximum(
                    highest, jnp.max(product[:, :span].reshape(-1, 8, span), axis=0)
                )
        if following is not None:
            peak_next[...] = highest
        if current is None:
            return
        other, peer = z_peer(tile + 1)
        totals = jnp.sum(totals, axis=0, keepdims=True)
        moments = jnp.sum(moments, axis=0, keepdims=True)
        share = 1.0 / totals
        center = moments * share
        attended = sums[:HDIM, :span] * share
        tilted = (sums[HDIM:, :span] + sums[:HDIM, span:]) * share - center * attended
        stats = split3(peak + jnp.log(totals)) + split3(center)
        stats = jnp.concatenate(
            [s.astype(jnp.float32) for s in stats]
            + [jnp.zeros((STAT - len(stats), span), jnp.float32)],
            axis=0,
        )
        part_out[j, other, :HDIM] = attended.astype(jnp.bfloat16)
        part_out[j, other, HDIM : 2 * HDIM] = tilted.astype(jnp.bfloat16)
        part_out[j, other, 2 * HDIM :] = stats.astype(jnp.bfloat16)

        @pl.when(tile < zs - 1)
        def _():
            send(
                part_out.at[j, other],
                part_in.at[j, z],
                part_send.at[j],
                part_recv.at[j],
                peer,
            ).start()

    def combine(j):
        part_in[j, z] = part_out[j, z]
        if zs > 1:
            drain(part_in.at[j, pl.ds(0, zs - 1)], part_recv.at[j])
        logs, centers = [], []
        for b in range(zs):
            stats = part_in[j, b, 2 * HDIM :].astype(jnp.float32)
            logs.append(stats[0:1] + stats[1:2] + stats[2:3])
            centers.append(stats[3:4] + stats[4:5] + stats[5:6])
        top = functools.reduce(jnp.maximum, logs)
        shares = [jnp.exp(entry - top) for entry in logs]
        scale = 1.0 / functools.reduce(jnp.add, shares)
        shares = [entry * scale for entry in shares]
        middle = functools.reduce(jnp.add, [s * c for s, c in zip(shares, centers)])
        attended = jnp.zeros((HDIM, span), jnp.float32)
        tilted = jnp.zeros((HDIM, span), jnp.float32)
        for b in range(zs):
            piece = part_in[j, b, :HDIM].astype(jnp.float32) * shares[b]
            attended = attended + piece
            tilted = tilted + part_in[j, b, HDIM : 2 * HDIM].astype(jnp.float32) * shares[b]
            tilted = tilted + piece * (centers[b] - middle)
        result = jnp.concatenate([attended, tilted], axis=0)
        for y in range(ys):
            merged[j, y] = result[:, y * ROWS : (y + 1) * ROWS].T.astype(jnp.bfloat16)
        joined[group, yl, j, body] = merged[j, yl]

        def hand(source, target, peer):
            send(source, target, head_send.at[j], head_recv.at[j], peer).start()

        for peer, block in ((fellow, 1 - yl), (diagonal, 1 - yl), (partner, yl)):
            hand(merged.at[j, block], joined.at[group, yl, j, body], peer)
        for y in range(ys):
            ctx = ctx_of(z, x, y, core)
            for g in (group, 1 - group):
                hand(
                    merged.at[j, y, pl.ds(0, MARGIN)],
                    joined.at[group, yl, j, pl.ds(MARGIN + ROWS, MARGIN)],
                    (before(ctx), g),
                )
                hand(
                    merged.at[j, y, pl.ds(ROWS - MARGIN, MARGIN)],
                    joined.at[group, yl, j, pl.ds(0, MARGIN)],
                    (after(ctx), g),
                )

    def prepare(u):
        j, tile = tile_of(u)
        other, _ = z_peer(tile + 1)

        @pl.when(u < away)
        def _():
            drain(qq.at[j, pl.ds(other * ys, ys)], q_recv.at[j, other])

        @pl.when(tile == 0)
        def _():
            for step in range(xs):
                source = lax.rem(x + step, xs)
                drain(kv.at[j, pl.ds(slot(source, 1 - core, 0), ys)], sibling_recv.at[j, source])

        @pl.when(jnp.logical_and(tile == max(zs - 2, 0), j < own - 1))
        def _():
            forward(j + 1)

    even, odd = (product_even, peak_even), (product_odd, peak_odd)

    prepare(0)
    work(None, 0, *odd, *even)

    @pl.loop(0, tiles // 2 - 1)
    def _(pair):
        u = 2 * pair
        prepare(u + 1)
        work(u, u + 1, *even, *odd)
        prepare(u + 2)
        work(u + 1, u + 2, *odd, *even)

    for j in range(own - 2):
        combine(j)
    prepare(tiles - 1)
    work(tiles - 2, tiles - 1, *even, *odd)
    combine(own - 2)
    work(tiles - 1, None, *odd, *even)
    combine(own - 1)

    low = lax.broadcasted_iota(jnp.int32, (ROWS + 2 * MARGIN, 2 * HDIM), 1) < HDIM

    def project_out(j):
        drain(merged.at[pl.ds(0, 2)], head_recv.at[j])
        outs, slopes, weights = [], [], []
        for g in range(2):
            first = joined[g, 0, j].astype(jnp.float32)
            second = joined[g, 1, j].astype(jnp.float32)
            outs.append(jnp.where(low, first, pltpu.roll(second, HDIM, 1)))
            slopes.append(jnp.where(low, pltpu.roll(first, HDIM, 1), second))
            for y in range(ys):
                weights.append(wo_all[g, pl.ds((y * own + j) * HDIM, HDIM)])
        rows = jnp.concatenate(
            [jnp.concatenate(outs, axis=1), jnp.concatenate(slopes, axis=1)], axis=0
        )
        return jnp.dot(
            rows.astype(jnp.bfloat16),
            jnp.concatenate(weights, axis=0),
            preferred_element_type=jnp.float32,
        )

    wo_copy.wait()
    to_right.wait()
    to_left.wait()
    mixing = functools.reduce(jnp.add, [project_out(j) for j in range(own)])
    length = ROWS + 2 * MARGIN
    for which in range(2):
        mixed = inputs[which].astype(jnp.float32) + mixing[which * length : (which + 1) * length]
        wide[which] = mixed.astype(jnp.bfloat16).astype(jnp.float32)

    for load in loads[7:]:
        load.wait()
    taps = taps_ref.shape[0]
    reach = MARGIN - taps // 2
    for chunk in range(wide.shape[2] // 128):
        cols = slice(chunk * 128, (chunk + 1) * 128)
        weights = taps_ref[:, cols]
        filtered = []
        for which in range(2):
            total = jnp.zeros((ROWS, 128), jnp.float32)
            for phase in range(8):
                partial = None
                for tap in range(phase, taps, 8):
                    start = tap - phase
                    term = weights[tap : tap + 1] * wide[which, start : start + ROWS + 8, cols]
                    partial = term if partial is None else partial + term
                total = total + partial[phase + reach : phase + reach + ROWS]
            filtered.append(total)
        preact = filtered[0] + bias_ref[cols].reshape(1, -1)
        gating = 1.0 / (1.0 + jnp.exp(-preact))
        act[:ROWS, cols] = (preact * gating).astype(jnp.bfloat16)
        act[ROWS:, cols] = (
            gating * (1.0 + preact * (1.0 - gating)) * filtered[1]
        ).astype(jnp.bfloat16)

    total = jnp.dot(act[...], wm_ref[...], preferred_element_type=jnp.float32)
    own_cols = pl.ds(pl.multiple_of(group * half, 128), half)
    out_ref[...] = (wide[0, body, own_cols] + total[:ROWS]).astype(jnp.bfloat16)
    slope_ref[...] = (wide[1, body, own_cols] + total[ROWS:]).astype(jnp.bfloat16)

    for j in range(own):
        drain(kv.at[j, pl.ds(0, 2 * ys * (xs - 1) + ys)], kv_send.at[j])
        if zs > 1:
            drain(qq.at[j, pl.ds(0, ys * (zs - 1))], q_send.at[j])
            drain(part_out.at[j, pl.ds(0, zs - 1)], part_send.at[j])
        drain(merged.at[pl.ds(0, 2)], head_send.at[j])


def shards(
    sizes,
    frames,
    tangent,
    norm_gain,
    query_weight,
    key_weight,
    value_weight,
    out_weight,
    conv_weight,
    conv_bias,
    mix_weight,
):
    zs, xs, ys, cs = sizes
    width, half = query_weight.shape
    heads = half // HDIM
    own = heads // ys
    nk = xs * cs * ys
    length = ROWS + 2 * MARGIN
    sem = pltpu.SemaphoreType.DMA
    hbm = pl.BlockSpec(memory_space=pl.ANY)
    vmem = pl.BlockSpec(memory_space=pltpu.VMEM)
    shape = jax.ShapeDtypeStruct((ROWS, half), jnp.bfloat16)
    operands = (
        frames,
        tangent,
        norm_gain,
        query_weight,
        key_weight,
        value_weight,
        out_weight,
        conv_weight,
        conv_bias,
        mix_weight,
    )
    part = (own, zs, 2 * HDIM + STAT, ys * ROWS)
    return pl.pallas_call(
        functools.partial(kernel, sizes, heads),
        out_shape=(shape, shape),
        in_specs=[hbm] * len(operands),
        out_specs=(vmem, vmem),
        scratch_shapes=[
            pltpu.VMEM((2, length, width), jnp.bfloat16),
            pltpu.VMEM((width,), jnp.float32),
            pltpu.VMEM((width, half), jnp.bfloat16),
            pltpu.VMEM((width, half), jnp.bfloat16),
            pltpu.VMEM((width, half), jnp.bfloat16),
            pltpu.VMEM((2, half, width), jnp.bfloat16),
            pltpu.VMEM(conv_weight.shape, jnp.float32),
            pltpu.VMEM((width,), jnp.float32),
            pltpu.VMEM((width, half), jnp.bfloat16),
            pltpu.VMEM((ys, own, 2, ROWS, 2 * HDIM), jnp.bfloat16),
            pltpu.VMEM((ys, own, 2 * HDIM, ROWS), jnp.bfloat16),
            pltpu.VMEM((own, nk, 2, ROWS, 2 * HDIM), jnp.bfloat16),
            pltpu.VMEM((own, zs * ys, 2 * HDIM, ROWS), jnp.bfloat16),
            pltpu.VMEM(part, jnp.bfloat16),
            pltpu.VMEM(part, jnp.bfloat16),
            pltpu.VMEM((own, ys, ROWS, 2 * HDIM), jnp.bfloat16),
            pltpu.VMEM((2, ys, own, length, 2 * HDIM), jnp.bfloat16),
            pltpu.VMEM((2, length, width), jnp.float32),
            pltpu.VMEM((2 * ROWS, width), jnp.bfloat16),
            pltpu.VMEM((nk * ROWS, 2 * ys * ROWS), jnp.float32),
            pltpu.VMEM((nk * ROWS, 2 * ys * ROWS), jnp.float32),
            pltpu.VMEM((nk * ROWS, 2 * ys * ROWS), jnp.bfloat16),
            pltpu.VMEM((8, ys * ROWS), jnp.float32),
            pltpu.VMEM((8, ys * ROWS), jnp.float32),
            sem((len(operands),)),
            sem((2, own)),
            sem((2, own)),
            sem((own,)),
            sem((own, xs, ys)),
            sem((own, xs)),
            sem((own,)),
            sem((own, zs)),
            sem((own,)),
            sem((own,)),
            sem((own,)),
            sem((own,)),
            sem((2,)),
            sem((4,)),
        ],
        compiler_params=pltpu.CompilerParams(
            collective_id=0, has_side_effects=True, vmem_limit_bytes=60 * 1024 * 1024
        ),
        name="block",
    )(*operands)


def solution(mesh):
    sizes = FACTORS[mesh.shape["ctx"]]
    placed = (
        P("ctx", None),
        P("ctx", None),
        P(),
        P(None, "head"),
        P(None, "head"),
        P(None, "head"),
        P("head", None),
        P(),
        P(),
        P(None, "head"),
    )
    return jax.shard_map(
        functools.partial(shards, sizes),
        mesh=mesh,
        in_specs=placed,
        out_specs=(P("ctx", "head"), P("ctx", "head")),
        check_vma=False,
    )
```

```python
import functools

import jax
import jax.numpy as jnp
from jax import lax
from jax.experimental import pallas as pl
from jax.experimental.pallas import tpu as pltpu
from jax.sharding import PartitionSpec as P

MESH = pl.DeviceIdType.MESH
HDIM = 64
EPSILON = 1e-06
ROWS = 128
STAT = 16
MARGIN = 16
FACTORS = {64: (4, 4, 2, 2)}


def split3(value):
    first = value.astype(jnp.bfloat16)
    rest = value - first.astype(jnp.float32)
    second = rest.astype(jnp.bfloat16)
    third = (rest - second.astype(jnp.float32)).astype(jnp.bfloat16)
    return [first, second, third]


def kernel(
    sizes,
    heads,
    frames_hbm,
    tangent_hbm,
    gain_hbm,
    wq_hbm,
    wk_hbm,
    wv_hbm,
    wo_hbm,
    taps_hbm,
    bias_hbm,
    wm_hbm,
    out_ref,
    inputs,
    gain_ref,
    wq_ref,
    wk_ref,
    wv_ref,
    wo_all,
    taps_ref,
    bias_ref,
    wm_ref,
    stage_kv,
    stage_q,
    kv,
    qq,
    part_out,
    part_in,
    merged,
    joined,
    wide,
    act,
    product_even,
    product_odd,
    chances,
    peak_even,
    peak_odd,
    load_sem,
    relay_sem,
    relay_q_sem,
    kv_send,
    direct_recv,
    sibling_recv,
    q_send,
    q_recv,
    part_send,
    part_recv,
    head_send,
    head_recv,
    wo_sem,
    halo_sem,
):
    zs, xs, ys, cs = sizes
    count = zs * xs * ys * cs
    half = heads * HDIM
    own = heads // ys
    nk = xs * cs * ys
    span = ys * ROWS
    me = lax.axis_index("ctx")
    group = lax.axis_index("head")
    core = lax.rem(me, cs)
    yl = lax.rem(me // cs, ys)
    x = lax.rem(me // (cs * ys), xs)
    z = me // (cs * ys * xs)

    def ctx_of(z_, x_, y_, c_):
        return ((z_ * xs + x_) * ys + y_) * cs + c_

    sibling = (ctx_of(z, x, yl, 1 - core), group)
    fellow = (ctx_of(z, x, 1 - yl, core), group)
    partner = (me, 1 - group)
    diagonal = (ctx_of(z, x, 1 - yl, core), 1 - group)

    def after(ctx):
        return lax.rem(ctx + 1, count)

    def before(ctx):
        return lax.rem(ctx + count - 1, count)

    right, left = (after(me), group), (before(me), group)
    x_peers = []
    for step in sorted(range(1, xs), key=lambda step: min(step, xs - step)):
        other = lax.rem(x + step, xs)
        x_peers.append((other, (ctx_of(z, other, yl, core), group)))

    def z_peer(step):
        other = lax.rem(z + step, zs)
        return other, (ctx_of(other, x, yl, core), group)

    z_peers = [z_peer(step) for step in range(1, zs)]

    loads = []
    body = pl.ds(MARGIN, ROWS)
    for source, target in (
        (frames_hbm, inputs.at[0, body]),
        (tangent_hbm, inputs.at[1, body]),
        (gain_hbm, gain_ref),
        (wk_hbm, wk_ref),
        (wv_hbm, wv_ref),
        (wq_hbm, wq_ref),
        (wo_hbm, wo_all.at[group]),
        (wm_hbm, wm_ref),
        (taps_hbm, taps_ref),
        (bias_hbm, bias_ref),
    ):
        load = pltpu.make_async_copy(source, target, load_sem.at[len(loads)])
        load.start()
        loads.append(load)

    barrier = pltpu.get_barrier_semaphore()
    everyone = []
    near_square = lax.rem(z * xs + x + zs * xs + 2 * core - 1, zs * xs)
    for g in (group, 1 - group):
        for y in (yl, 1 - yl):
            everyone += [(ctx_of(z, x, y, core), g), (ctx_of(z, x, y, 1 - core), g)]
            everyone.append(((near_square * ys + y) * cs + 1 - core, g))
    everyone = everyone[1:]
    everyone += [peer for _, peer in x_peers] + [peer for _, peer in z_peers]
    for peer in everyone:
        pl.semaphore_signal(barrier, inc=1, device_id=peer, device_id_type=MESH)

    def send(source, target, send_sem, recv_sem, peer):
        return pltpu.make_async_remote_copy(
            src_ref=source,
            dst_ref=target,
            send_sem=send_sem,
            recv_sem=recv_sem,
            device_id=peer,
            device_id_type=MESH,
        )

    def drain(ref, sem):
        pltpu.make_async_copy(ref, ref, sem).wait()

    for load in loads[:3]:
        load.wait()
    plain = inputs[0, body].astype(jnp.float32)
    slope = inputs[1, body].astype(jnp.float32)
    gain = gain_ref[...].reshape(1, -1)
    inverse = lax.rsqrt(jnp.mean(plain * plain, axis=-1, keepdims=True) + EPSILON)
    cross = jnp.mean(plain * slope, axis=-1, keepdims=True)
    normed = (plain * inverse * gain).astype(jnp.bfloat16)
    normed_slope = (
        gain * (slope * inverse - plain * inverse * inverse * inverse * cross)
    ).astype(jnp.bfloat16)
    both = jnp.concatenate([normed, normed_slope], axis=0)

    def project(weight_ref):
        return jnp.dot(both, weight_ref[...], preferred_element_type=jnp.float32)

    loads[3].wait()
    keys = project(wk_ref)
    low = lax.broadcasted_iota(jnp.int32, (ROWS, 2 * HDIM), 1) < HDIM
    for pair in range(heads // 2):
        cols = slice(pair * 2 * HDIM, (pair + 1) * 2 * HDIM)
        key_pair, slope_pair = keys[:ROWS, cols], keys[ROWS:, cols]
        even = jnp.where(low, key_pair, pltpu.roll(slope_pair, HDIM, 1))
        odd = jnp.where(low, pltpu.roll(key_pair, HDIM, 1), slope_pair)
        for h, value in ((2 * pair, even), (2 * pair + 1, odd)):
            stage_kv[h // own, h % own, 0] = value.astype(jnp.bfloat16)

    def turned(values):
        return (
            values[:ROWS].T.astype(jnp.bfloat16),
            values[ROWS:].T.astype(jnp.bfloat16),
        )

    loads[4].wait()
    values, value_slope = turned(project(wv_ref))
    for h in range(heads):
        rows = slice(h * HDIM, (h + 1) * HDIM)
        stage_kv[h // own, h % own, 1, :HDIM] = values[rows]
        stage_kv[h // own, h % own, 1, HDIM:] = value_slope[rows]

    pl.semaphore_wait(barrier, len(everyone))

    def slot(x_, c_, y_):
        return (x_ * cs + c_) * ys + y_

    def relay_kv(j):
        return send(
            stage_kv.at[1 - yl, j],
            kv.at[j, slot(x, core, yl)],
            relay_sem.at[0, j],
            relay_sem.at[1, j],
            fellow,
        )

    def relay_q(j):
        return send(
            stage_q.at[1 - yl, j],
            qq.at[j, z * ys + yl],
            relay_q_sem.at[0, j],
            relay_q_sem.at[1, j],
            fellow,
        )

    def direct(j, which, peer):
        here = kv.at[j, slot(x, core, which)]
        return send(here, here, kv_send.at[j], direct_recv.at[j, x, which], peer)

    def pass_on(j, source):
        here = kv.at[j, pl.ds(slot(source, core, 0), ys)]
        return send(here, here, kv_send.at[j], sibling_recv.at[j, source], sibling)

    def spread(j, which):
        for _, peer in x_peers:
            direct(j, which, peer).start()

    for j in range(own):
        relay_kv(j).start()
        if j == 0:
            kv[0, slot(x, core, yl)] = stage_kv[yl, 0]
            spread(0, yl)

    loads[5].wait()
    queries, query_slope = turned(project(wq_ref))
    queries, query_slope = queries * 0.125, query_slope * 0.125
    for h in range(heads):
        rows = slice(h * HDIM, (h + 1) * HDIM)
        stage_q[h // own, h % own, :HDIM] = queries[rows]
        stage_q[h // own, h % own, HDIM:] = query_slope[rows]
    for j in range(own):
        relay_q(j).start()
    for j in range(own):
        if j > 0:
            kv[j, slot(x, core, yl)] = stage_kv[yl, j]
        qq[j, z * ys + yl] = stage_q[yl, j]

    def relay(j):
        relay_kv(j).wait()
        spread(j, 1 - yl)
        pass_on(j, x).start()
        relay_q(j).wait()
        here = qq.at[j, pl.ds(z * ys, ys)]
        for _, peer in z_peers:
            send(here, here, q_send.at[j], q_recv.at[j, z], peer).start()
        if j < own - 1:
            spread(j + 1, yl)

    def forward(j):
        for other, _ in x_peers:
            for which in range(ys):
                drain(kv.at[j, slot(other, core, which)], direct_recv.at[j, other, which])
            pass_on(j, other).start()

    for j in range(own):
        relay(j)
    forward(0)
    loads[6].wait()
    here = wo_all.at[group]
    wo_copy = send(here, here, wo_sem.at[0], wo_sem.at[1], partner)
    wo_copy.start()
    to_right = send(
        inputs.at[:, pl.ds(ROWS, MARGIN)],
        inputs.at[:, pl.ds(0, MARGIN)],
        halo_sem.at[0],
        halo_sem.at[1],
        right,
    )
    to_left = send(
        inputs.at[:, pl.ds(MARGIN, MARGIN)],
        inputs.at[:, pl.ds(ROWS + MARGIN, MARGIN)],
        halo_sem.at[2],
        halo_sem.at[3],
        left,
    )
    to_right.start()
    to_left.start()

    tiles = own * zs
    chunk_rows = min(512, nk * ROWS)
    chunk_blocks = chunk_rows // ROWS
    step_rows = 64

    away = own * (zs - 1)

    def tile_of(u):
        if zs == 1:
            return u, 0
        early = u < away
        j = jnp.where(early, u // (zs - 1), u - away)
        return j, jnp.where(early, lax.rem(u, zs - 1), zs - 1)

    def queries_of(u):
        j, tile = tile_of(u)
        other, _ = z_peer(tile + 1)
        blocks = [qq[j, other * ys + y] for y in range(ys)]
        plain_q = jnp.concatenate([block[:HDIM] for block in blocks], axis=1)
        slope_q = jnp.concatenate([block[HDIM:] for block in blocks], axis=1)
        top = jnp.concatenate([plain_q, slope_q], axis=1)
        bottom = jnp.concatenate([jnp.zeros_like(plain_q), plain_q], axis=1)
        return jnp.concatenate([top, bottom], axis=0)

    def work(current, following, product_now, peak_now, product_next, peak_next):
        if current is not None:
            j, tile = tile_of(current)
            peak = jnp.max(peak_now[...], axis=0, keepdims=True)
            totals = jnp.zeros((8, span), jnp.float32)
            moments = jnp.zeros((8, span), jnp.float32)
            sums = None
        if following is not None:
            next_j, _ = tile_of(following)
            next_queries = queries_of(following)
            highest = jnp.full((8, span), -jnp.inf, jnp.float32)
        for first in range(0, nk, chunk_blocks):
            chunk = slice(first * ROWS, (first + chunk_blocks) * ROWS)
            if current is not None:
                for start in range(chunk.start, chunk.stop, step_rows):
                    rows = slice(start, start + step_rows)
                    weights = jnp.exp(product_now[rows, :span] - peak)
                    slanted = weights * product_now[rows, span:]
                    totals = totals + jnp.sum(weights.reshape(-1, 8, span), axis=0)
                    moments = moments + jnp.sum(slanted.reshape(-1, 8, span), axis=0)
                    chances[rows, :span] = weights.astype(jnp.bfloat16)
                    chances[rows, span:] = slanted.astype(jnp.bfloat16)
                value_cols = jnp.concatenate(
                    [kv[j, first + b, 1] for b in range(chunk_blocks)], axis=1
                )
                part = jnp.dot(value_cols, chances[chunk], preferred_element_type=jnp.float32)
                sums = part if sums is None else sums + part
            if following is not None:
                key_rows = kv[next_j, pl.ds(first, chunk_blocks), 0].reshape(chunk_rows, 2 * HDIM)
                product = jnp.dot(key_rows, next_queries, preferred_element_type=jnp.float32)
                product_next[chunk] = product
                highest = jnp.maximum(
                    highest, jnp.max(product[:, :span].reshape(-1, 8, span), axis=0)
                )
        if following is not None:
            peak_next[...] = highest
        if current is None:
            return
        other, peer = z_peer(tile + 1)
        totals = jnp.sum(totals, axis=0, keepdims=True)
        moments = jnp.sum(moments, axis=0, keepdims=True)
        share = 1.0 / totals
        center = moments * share
        attended = sums[:HDIM, :span] * share
        tilted = (sums[HDIM:, :span] + sums[:HDIM, span:]) * share - center * attended
        stats = split3(peak + jnp.log(totals)) + split3(center)
        stats = jnp.concatenate(
            [s.astype(jnp.float32) for s in stats]
            + [jnp.zeros((STAT - len(stats), span), jnp.float32)],
            axis=0,
        )
        part_out[j, other, :HDIM] = attended.astype(jnp.bfloat16)
        part_out[j, other, HDIM : 2 * HDIM] = tilted.astype(jnp.bfloat16)
        part_out[j, other, 2 * HDIM :] = stats.astype(jnp.bfloat16)

        @pl.when(tile < zs - 1)
        def _():
            send(
                part_out.at[j, other],
                part_in.at[j, z],
                part_send.at[j],
                part_recv.at[j],
                peer,
            ).start()

    def combine(j):
        part_in[j, z] = part_out[j, z]
        if zs > 1:
            drain(part_in.at[j, pl.ds(0, zs - 1)], part_recv.at[j])
        logs, centers = [], []
        for b in range(zs):
            stats = part_in[j, b, 2 * HDIM :].astype(jnp.float32)
            logs.append(stats[0:1] + stats[1:2] + stats[2:3])
            centers.append(stats[3:4] + stats[4:5] + stats[5:6])
        top = functools.reduce(jnp.maximum, logs)
        shares = [jnp.exp(entry - top) for entry in logs]
        scale = 1.0 / functools.reduce(jnp.add, shares)
        shares = [entry * scale for entry in shares]
        middle = functools.reduce(jnp.add, [s * c for s, c in zip(shares, centers)])
        attended = jnp.zeros((HDIM, span), jnp.float32)
        tilted = jnp.zeros((HDIM, span), jnp.float32)
        for b in range(zs):
            piece = part_in[j, b, :HDIM].astype(jnp.float32) * shares[b]
            attended = attended + piece
            tilted = tilted + part_in[j, b, HDIM : 2 * HDIM].astype(jnp.float32) * shares[b]
            tilted = tilted + piece * (centers[b] - middle)
        result = jnp.concatenate([attended, tilted], axis=0)
        for y in range(ys):
            merged[j, y] = result[:, y * ROWS : (y + 1) * ROWS].T.astype(jnp.bfloat16)
        joined[group, yl, j, body] = merged[j, yl]

        def hand(source, target, peer):
            send(source, target, head_send.at[j], head_recv.at[j], peer).start()

        for y in range(ys):
            ctx = ctx_of(z, x, y, core)
            for g in (group, 1 - group):
                hand(
                    merged.at[j, y, pl.ds(0, MARGIN)],
                    joined.at[group, yl, j, pl.ds(MARGIN + ROWS, MARGIN)],
                    (before(ctx), g),
                )
                hand(
                    merged.at[j, y, pl.ds(ROWS - MARGIN, MARGIN)],
                    joined.at[group, yl, j, pl.ds(0, MARGIN)],
                    (after(ctx), g),
                )
        for peer, block in ((fellow, 1 - yl), (diagonal, 1 - yl), (partner, yl)):
            hand(merged.at[j, block], joined.at[group, yl, j, body], peer)

    def prepare(u):
        j, tile = tile_of(u)
        other, _ = z_peer(tile + 1)

        @pl.when(u < away)
        def _():
            drain(qq.at[j, pl.ds(other * ys, ys)], q_recv.at[j, other])

        @pl.when(tile == 0)
        def _():
            for step in range(xs):
                source = lax.rem(x + step, xs)
                drain(kv.at[j, pl.ds(slot(source, 1 - core, 0), ys)], sibling_recv.at[j, source])

        @pl.when(jnp.logical_and(tile == max(zs - 2, 0), j < own - 1))
        def _():
            forward(j + 1)

    even, odd = (product_even, peak_even), (product_odd, peak_odd)

    prepare(0)
    work(None, 0, *odd, *even)

    @pl.loop(0, tiles // 2 - 1)
    def _(pair):
        u = 2 * pair
        prepare(u + 1)
        work(u, u + 1, *even, *odd)
        prepare(u + 2)
        work(u + 1, u + 2, *odd, *even)

    for j in range(own - 2):
        combine(j)
    prepare(tiles - 1)
    work(tiles - 2, tiles - 1, *even, *odd)
    combine(own - 2)
    work(tiles - 1, None, *odd, *even)
    combine(own - 1)

    low = lax.broadcasted_iota(jnp.int32, (ROWS + 2 * MARGIN, 2 * HDIM), 1) < HDIM

    def project_out(j):
        drain(merged.at[pl.ds(0, 2)], head_recv.at[j])
        outs, slopes, weights = [], [], []
        for g in range(2):
            first = joined[g, 0, j].astype(jnp.float32)
            second = joined[g, 1, j].astype(jnp.float32)
            outs.append(jnp.where(low, first, pltpu.roll(second, HDIM, 1)))
            slopes.append(jnp.where(low, pltpu.roll(first, HDIM, 1), second))
            for y in range(ys):
                weights.append(wo_all[g, pl.ds((y * own + j) * HDIM, HDIM)])
        rows = jnp.concatenate(
            [jnp.concatenate(outs, axis=1), jnp.concatenate(slopes, axis=1)], axis=0
        )
        return jnp.dot(
            rows.astype(jnp.bfloat16),
            jnp.concatenate(weights, axis=0),
            preferred_element_type=jnp.float32,
        )

    wo_copy.wait()
    to_right.wait()
    to_left.wait()
    mixing = functools.reduce(jnp.add, [project_out(j) for j in range(own)])
    length = ROWS + 2 * MARGIN
    for which in range(2):
        mixed = inputs[which].astype(jnp.float32) + mixing[which * length : (which + 1) * length]
        wide[which] = mixed.astype(jnp.bfloat16).astype(jnp.float32)

    for load in loads[7:]:
        load.wait()
    taps = taps_ref.shape[0]
    reach = MARGIN - taps // 2
    for chunk in range(wide.shape[2] // 128):
        cols = slice(chunk * 128, (chunk + 1) * 128)
        weights = taps_ref[:, cols]
        filtered = []
        for which in range(2):
            total = jnp.zeros((ROWS, 128), jnp.float32)
            for phase in range(8):
                partial = None
                for tap in range(phase, taps, 8):
                    start = tap - phase
                    term = weights[tap : tap + 1] * wide[which, start : start + ROWS + 8, cols]
                    partial = term if partial is None else partial + term
                total = total + partial[phase + reach : phase + reach + ROWS]
            filtered.append(total)
        preact = filtered[0] + bias_ref[cols].reshape(1, -1)
        gating = 1.0 / (1.0 + jnp.exp(-preact))
        act[:ROWS, cols] = (preact * gating).astype(jnp.bfloat16)
        act[ROWS:, cols] = (
            gating * (1.0 + preact * (1.0 - gating)) * filtered[1]
        ).astype(jnp.bfloat16)

    total = jnp.dot(act[...], wm_ref[...], preferred_element_type=jnp.float32)
    own_cols = pl.ds(pl.multiple_of(group * half, 128), half)
    out_ref[0] = (wide[0, body, own_cols] + total[:ROWS]).astype(jnp.bfloat16)
    out_ref[1] = (wide[1, body, own_cols] + total[ROWS:]).astype(jnp.bfloat16)

    for j in range(own):
        drain(kv.at[j, pl.ds(0, 2 * ys * (xs - 1) + ys)], kv_send.at[j])
        if zs > 1:
            drain(qq.at[j, pl.ds(0, ys * (zs - 1))], q_send.at[j])
            drain(part_out.at[j, pl.ds(0, zs - 1)], part_send.at[j])
        drain(merged.at[pl.ds(0, 2)], head_send.at[j])


def shards(
    sizes,
    frames,
    tangent,
    norm_gain,
    query_weight,
    key_weight,
    value_weight,
    out_weight,
    conv_weight,
    conv_bias,
    mix_weight,
):
    zs, xs, ys, cs = sizes
    width, half = query_weight.shape
    heads = half // HDIM
    own = heads // ys
    nk = xs * cs * ys
    length = ROWS + 2 * MARGIN
    sem = pltpu.SemaphoreType.DMA
    hbm = pl.BlockSpec(memory_space=pl.ANY)
    vmem = pl.BlockSpec(memory_space=pltpu.VMEM)
    shape = jax.ShapeDtypeStruct((2, ROWS, half), jnp.bfloat16)
    operands = (
        frames,
        tangent,
        norm_gain,
        query_weight,
        key_weight,
        value_weight,
        out_weight,
        conv_weight,
        conv_bias,
        mix_weight,
    )
    part = (own, zs, 2 * HDIM + STAT, ys * ROWS)
    both = pl.pallas_call(
        functools.partial(kernel, sizes, heads),
        out_shape=shape,
        in_specs=[hbm] * len(operands),
        out_specs=vmem,
        scratch_shapes=[
            pltpu.VMEM((2, length, width), jnp.bfloat16),
            pltpu.VMEM((width,), jnp.float32),
            pltpu.VMEM((width, half), jnp.bfloat16),
            pltpu.VMEM((width, half), jnp.bfloat16),
            pltpu.VMEM((width, half), jnp.bfloat16),
            pltpu.VMEM((2, half, width), jnp.bfloat16),
            pltpu.VMEM(conv_weight.shape, jnp.float32),
            pltpu.VMEM((width,), jnp.float32),
            pltpu.VMEM((width, half), jnp.bfloat16),
            pltpu.VMEM((ys, own, 2, ROWS, 2 * HDIM), jnp.bfloat16),
            pltpu.VMEM((ys, own, 2 * HDIM, ROWS), jnp.bfloat16),
            pltpu.VMEM((own, nk, 2, ROWS, 2 * HDIM), jnp.bfloat16),
            pltpu.VMEM((own, zs * ys, 2 * HDIM, ROWS), jnp.bfloat16),
            pltpu.VMEM(part, jnp.bfloat16),
            pltpu.VMEM(part, jnp.bfloat16),
            pltpu.VMEM((own, ys, ROWS, 2 * HDIM), jnp.bfloat16),
            pltpu.VMEM((2, ys, own, length, 2 * HDIM), jnp.bfloat16),
            pltpu.VMEM((2, length, width), jnp.float32),
            pltpu.VMEM((2 * ROWS, width), jnp.bfloat16),
            pltpu.VMEM((nk * ROWS, 2 * ys * ROWS), jnp.float32),
            pltpu.VMEM((nk * ROWS, 2 * ys * ROWS), jnp.float32),
            pltpu.VMEM((nk * ROWS, 2 * ys * ROWS), jnp.bfloat16),
            pltpu.VMEM((8, ys * ROWS), jnp.float32),
            pltpu.VMEM((8, ys * ROWS), jnp.float32),
            sem((len(operands),)),
            sem((2, own)),
            sem((2, own)),
            sem((own,)),
            sem((own, xs, ys)),
            sem((own, xs)),
            sem((own,)),
            sem((own, zs)),
            sem((own,)),
            sem((own,)),
            sem((own,)),
            sem((own,)),
            sem((2,)),
            sem((4,)),
        ],
        compiler_params=pltpu.CompilerParams(
            collective_id=0, has_side_effects=True, vmem_limit_bytes=60 * 1024 * 1024
        ),
        name="block",
    )(*operands)
    return both[0], both[1]


def solution(mesh):
    sizes = FACTORS[mesh.shape["ctx"]]
    placed = (
        P("ctx", None),
        P("ctx", None),
        P(),
        P(None, "head"),
        P(None, "head"),
        P(None, "head"),
        P("head", None),
        P(),
        P(),
        P(None, "head"),
    )
    return jax.shard_map(
        functools.partial(shards, sizes),
        mesh=mesh,
        in_specs=placed,
        out_specs=(P("ctx", "head"), P("ctx", "head")),
        check_vma=False,
    )
```

```python
import functools

import jax
import jax.numpy as jnp
from jax import lax
from jax.experimental import pallas as pl
from jax.experimental.pallas import tpu as pltpu
from jax.sharding import PartitionSpec as P

MESH = pl.DeviceIdType.MESH
HDIM = 64
EPSILON = 1e-06
ROWS = 128
STAT = 16
MARGIN = 16
FACTORS = {64: (4, 4, 2, 2)}


def split3(value):
    first = value.astype(jnp.bfloat16)
    rest = value - first.astype(jnp.float32)
    second = rest.astype(jnp.bfloat16)
    third = (rest - second.astype(jnp.float32)).astype(jnp.bfloat16)
    return [first, second, third]


def kernel(
    sizes,
    heads,
    frames_hbm,
    tangent_hbm,
    gain_hbm,
    wq_hbm,
    wk_hbm,
    wv_hbm,
    wo_hbm,
    taps_hbm,
    bias_hbm,
    wm_hbm,
    out_ref,
    inputs,
    gain_ref,
    wq_ref,
    wk_ref,
    wv_ref,
    wo_all,
    taps_ref,
    bias_ref,
    wm_ref,
    stage_kv,
    stage_q,
    kv,
    qq,
    part_out,
    part_in,
    merged,
    joined,
    wide,
    act,
    product_even,
    product_odd,
    chances,
    peak_even,
    peak_odd,
    load_sem,
    relay_sem,
    relay_q_sem,
    kv_send,
    direct_recv,
    sibling_recv,
    q_send,
    q_recv,
    part_send,
    part_recv,
    head_send,
    head_recv,
    wo_sem,
    halo_sem,
):
    zs, xs, ys, cs = sizes
    count = zs * xs * ys * cs
    half = heads * HDIM
    own = heads // ys
    nk = xs * cs * ys
    span = ys * ROWS
    me = lax.axis_index("ctx")
    group = lax.axis_index("head")
    core = lax.rem(me, cs)
    yl = lax.rem(me // cs, ys)
    x = lax.rem(me // (cs * ys), xs)
    z = me // (cs * ys * xs)

    def ctx_of(z_, x_, y_, c_):
        return ((z_ * xs + x_) * ys + y_) * cs + c_

    sibling = (ctx_of(z, x, yl, 1 - core), group)
    fellow = (ctx_of(z, x, 1 - yl, core), group)
    partner = (me, 1 - group)
    diagonal = (ctx_of(z, x, 1 - yl, core), 1 - group)

    def after(ctx):
        return lax.rem(ctx + 1, count)

    def before(ctx):
        return lax.rem(ctx + count - 1, count)

    right, left = (after(me), group), (before(me), group)
    x_peers = []
    for step in sorted(range(1, xs), key=lambda step: min(step, xs - step)):
        other = lax.rem(x + step, xs)
        x_peers.append((other, (ctx_of(z, other, yl, core), group)))

    def z_peer(step):
        other = lax.rem(z + step, zs)
        return other, (ctx_of(other, x, yl, core), group)

    z_peers = [z_peer(step) for step in range(1, zs)]

    loads = []
    body = pl.ds(MARGIN, ROWS)
    for source, target in (
        (frames_hbm, inputs.at[0, body]),
        (tangent_hbm, inputs.at[1, body]),
        (gain_hbm, gain_ref),
        (wk_hbm, wk_ref),
        (wv_hbm, wv_ref),
        (wq_hbm, wq_ref),
        (wo_hbm, wo_all.at[group]),
        (wm_hbm, wm_ref),
        (taps_hbm, taps_ref),
        (bias_hbm, bias_ref),
    ):
        load = pltpu.make_async_copy(source, target, load_sem.at[len(loads)])
        load.start()
        loads.append(load)

    barrier = pltpu.get_barrier_semaphore()
    everyone = []
    near_square = lax.rem(z * xs + x + zs * xs + 2 * core - 1, zs * xs)
    for g in (group, 1 - group):
        for y in (yl, 1 - yl):
            everyone += [(ctx_of(z, x, y, core), g), (ctx_of(z, x, y, 1 - core), g)]
            everyone.append(((near_square * ys + y) * cs + 1 - core, g))
    everyone = everyone[1:]
    everyone += [peer for _, peer in x_peers] + [peer for _, peer in z_peers]
    for peer in everyone:
        pl.semaphore_signal(barrier, inc=1, device_id=peer, device_id_type=MESH)

    def send(source, target, send_sem, recv_sem, peer):
        return pltpu.make_async_remote_copy(
            src_ref=source,
            dst_ref=target,
            send_sem=send_sem,
            recv_sem=recv_sem,
            device_id=peer,
            device_id_type=MESH,
        )

    def drain(ref, sem):
        pltpu.make_async_copy(ref, ref, sem).wait()

    for load in loads[:3]:
        load.wait()
    plain = inputs[0, body].astype(jnp.float32)
    slope = inputs[1, body].astype(jnp.float32)
    gain = gain_ref[...].reshape(1, -1)
    inverse = lax.rsqrt(jnp.mean(plain * plain, axis=-1, keepdims=True) + EPSILON)
    cross = jnp.mean(plain * slope, axis=-1, keepdims=True)
    normed = (plain * inverse * gain).astype(jnp.bfloat16)
    normed_slope = (
        gain * (slope * inverse - plain * inverse * inverse * inverse * cross)
    ).astype(jnp.bfloat16)
    both = jnp.concatenate([normed, normed_slope], axis=0)

    def project(weight_ref):
        return jnp.dot(both, weight_ref[...], preferred_element_type=jnp.float32)

    loads[3].wait()
    keys = project(wk_ref)
    low = lax.broadcasted_iota(jnp.int32, (ROWS, 2 * HDIM), 1) < HDIM
    for pair in range(heads // 2):
        cols = slice(pair * 2 * HDIM, (pair + 1) * 2 * HDIM)
        key_pair, slope_pair = keys[:ROWS, cols], keys[ROWS:, cols]
        even = jnp.where(low, key_pair, pltpu.roll(slope_pair, HDIM, 1))
        odd = jnp.where(low, pltpu.roll(key_pair, HDIM, 1), slope_pair)
        for h, value in ((2 * pair, even), (2 * pair + 1, odd)):
            stage_kv[h // own, h % own, 0] = value.astype(jnp.bfloat16)

    def turned(values):
        return (
            values[:ROWS].T.astype(jnp.bfloat16),
            values[ROWS:].T.astype(jnp.bfloat16),
        )

    loads[4].wait()
    values, value_slope = turned(project(wv_ref))
    for h in range(heads):
        rows = slice(h * HDIM, (h + 1) * HDIM)
        stage_kv[h // own, h % own, 1, :HDIM] = values[rows]
        stage_kv[h // own, h % own, 1, HDIM:] = value_slope[rows]

    pl.semaphore_wait(barrier, len(everyone))

    def slot(x_, c_, y_):
        return (x_ * cs + c_) * ys + y_

    def relay_kv(j):
        return send(
            stage_kv.at[1 - yl, j],
            kv.at[j, slot(x, core, yl)],
            relay_sem.at[0, j],
            relay_sem.at[1, j],
            fellow,
        )

    def relay_q(j):
        return send(
            stage_q.at[1 - yl, j],
            qq.at[j, z * ys + yl],
            relay_q_sem.at[0, j],
            relay_q_sem.at[1, j],
            fellow,
        )

    def direct(j, which, peer):
        here = kv.at[j, slot(x, core, which)]
        return send(here, here, kv_send.at[j], direct_recv.at[j, x, which], peer)

    def pass_on(j, source):
        here = kv.at[j, pl.ds(slot(source, core, 0), ys)]
        return send(here, here, kv_send.at[j], sibling_recv.at[j, source], sibling)

    def spread(j, which):
        for _, peer in x_peers:
            direct(j, which, peer).start()

    for j in range(own):
        relay_kv(j).start()
        if j == 0:
            kv[0, slot(x, core, yl)] = stage_kv[yl, 0]
            spread(0, yl)

    loads[5].wait()
    queries, query_slope = turned(project(wq_ref))
    queries, query_slope = queries * 0.125, query_slope * 0.125
    for h in range(heads):
        rows = slice(h * HDIM, (h + 1) * HDIM)
        stage_q[h // own, h % own, :HDIM] = queries[rows]
        stage_q[h // own, h % own, HDIM:] = query_slope[rows]
    for j in range(own):
        relay_q(j).start()
    for j in range(own):
        if j > 0:
            kv[j, slot(x, core, yl)] = stage_kv[yl, j]
        qq[j, z * ys + yl] = stage_q[yl, j]

    def relay(j):
        relay_kv(j).wait()
        spread(j, 1 - yl)
        pass_on(j, x).start()
        relay_q(j).wait()
        here = qq.at[j, pl.ds(z * ys, ys)]
        for _, peer in z_peers:
            send(here, here, q_send.at[j], q_recv.at[j, z], peer).start()
        if j < own - 1:
            spread(j + 1, yl)

    def forward(j):
        for other, _ in x_peers:
            for which in range(ys):
                drain(kv.at[j, slot(other, core, which)], direct_recv.at[j, other, which])
            pass_on(j, other).start()

    for j in range(own - 1):
        relay(j)
    forward(0)
    loads[6].wait()
    here = wo_all.at[group]
    wo_copy = send(here, here, wo_sem.at[0], wo_sem.at[1], partner)
    wo_copy.start()
    to_right = send(
        inputs.at[:, pl.ds(ROWS, MARGIN)],
        inputs.at[:, pl.ds(0, MARGIN)],
        halo_sem.at[0],
        halo_sem.at[1],
        right,
    )
    to_left = send(
        inputs.at[:, pl.ds(MARGIN, MARGIN)],
        inputs.at[:, pl.ds(ROWS + MARGIN, MARGIN)],
        halo_sem.at[2],
        halo_sem.at[3],
        left,
    )
    to_right.start()
    to_left.start()

    tiles = own * zs
    chunk_rows = min(512, nk * ROWS)
    chunk_blocks = chunk_rows // ROWS
    step_rows = 64

    away = own * (zs - 1)

    def tile_of(u):
        if zs == 1:
            return u, 0
        early = u < away
        j = jnp.where(early, u // (zs - 1), u - away)
        return j, jnp.where(early, lax.rem(u, zs - 1), zs - 1)

    def queries_of(u):
        j, tile = tile_of(u)
        other, _ = z_peer(tile + 1)
        blocks = [qq[j, other * ys + y] for y in range(ys)]
        plain_q = jnp.concatenate([block[:HDIM] for block in blocks], axis=1)
        slope_q = jnp.concatenate([block[HDIM:] for block in blocks], axis=1)
        top = jnp.concatenate([plain_q, slope_q], axis=1)
        bottom = jnp.concatenate([jnp.zeros_like(plain_q), plain_q], axis=1)
        return jnp.concatenate([top, bottom], axis=0)

    def work(current, following, product_now, peak_now, product_next, peak_next):
        if current is not None:
            j, tile = tile_of(current)
            peak = jnp.max(peak_now[...], axis=0, keepdims=True)
            totals = jnp.zeros((8, span), jnp.float32)
            moments = jnp.zeros((8, span), jnp.float32)
            sums = None
        if following is not None:
            next_j, _ = tile_of(following)
            next_queries = queries_of(following)
            highest = jnp.full((8, span), -jnp.inf, jnp.float32)
        for first in range(0, nk, chunk_blocks):
            chunk = slice(first * ROWS, (first + chunk_blocks) * ROWS)
            if current is not None:
                for start in range(chunk.start, chunk.stop, step_rows):
                    rows = slice(start, start + step_rows)
                    weights = jnp.exp(product_now[rows, :span] - peak)
                    slanted = weights * product_now[rows, span:]
                    totals = totals + jnp.sum(weights.reshape(-1, 8, span), axis=0)
                    moments = moments + jnp.sum(slanted.reshape(-1, 8, span), axis=0)
                    chances[rows, :span] = weights.astype(jnp.bfloat16)
                    chances[rows, span:] = slanted.astype(jnp.bfloat16)
                value_cols = jnp.concatenate(
                    [kv[j, first + b, 1] for b in range(chunk_blocks)], axis=1
                )
                part = jnp.dot(value_cols, chances[chunk], preferred_element_type=jnp.float32)
                sums = part if sums is None else sums + part
            if following is not None:
                key_rows = kv[next_j, pl.ds(first, chunk_blocks), 0].reshape(chunk_rows, 2 * HDIM)
                product = jnp.dot(key_rows, next_queries, preferred_element_type=jnp.float32)
                product_next[chunk] = product
                highest = jnp.maximum(
                    highest, jnp.max(product[:, :span].reshape(-1, 8, span), axis=0)
                )
        if following is not None:
            peak_next[...] = highest
        if current is None:
            return
        other, peer = z_peer(tile + 1)
        totals = jnp.sum(totals, axis=0, keepdims=True)
        moments = jnp.sum(moments, axis=0, keepdims=True)
        share = 1.0 / totals
        center = moments * share
        attended = sums[:HDIM, :span] * share
        tilted = (sums[HDIM:, :span] + sums[:HDIM, span:]) * share - center * attended
        stats = split3(peak + jnp.log(totals)) + split3(center)
        stats = jnp.concatenate(
            [s.astype(jnp.float32) for s in stats]
            + [jnp.zeros((STAT - len(stats), span), jnp.float32)],
            axis=0,
        )
        part_out[j, other, :HDIM] = attended.astype(jnp.bfloat16)
        part_out[j, other, HDIM : 2 * HDIM] = tilted.astype(jnp.bfloat16)
        part_out[j, other, 2 * HDIM :] = stats.astype(jnp.bfloat16)

        @pl.when(tile < zs - 1)
        def _():
            send(
                part_out.at[j, other],
                part_in.at[j, z],
                part_send.at[j],
                part_recv.at[j],
                peer,
            ).start()

    def combine(j):
        part_in[j, z] = part_out[j, z]
        if zs > 1:
            drain(part_in.at[j, pl.ds(0, zs - 1)], part_recv.at[j])
        logs, centers = [], []
        for b in range(zs):
            stats = part_in[j, b, 2 * HDIM :].astype(jnp.float32)
            logs.append(stats[0:1] + stats[1:2] + stats[2:3])
            centers.append(stats[3:4] + stats[4:5] + stats[5:6])
        top = functools.reduce(jnp.maximum, logs)
        shares = [jnp.exp(entry - top) for entry in logs]
        scale = 1.0 / functools.reduce(jnp.add, shares)
        shares = [entry * scale for entry in shares]
        middle = functools.reduce(jnp.add, [s * c for s, c in zip(shares, centers)])
        attended = jnp.zeros((HDIM, span), jnp.float32)
        tilted = jnp.zeros((HDIM, span), jnp.float32)
        for b in range(zs):
            piece = part_in[j, b, :HDIM].astype(jnp.float32) * shares[b]
            attended = attended + piece
            tilted = tilted + part_in[j, b, HDIM : 2 * HDIM].astype(jnp.float32) * shares[b]
            tilted = tilted + piece * (centers[b] - middle)
        result = jnp.concatenate([attended, tilted], axis=0)
        for y in range(ys):
            merged[j, y] = result[:, y * ROWS : (y + 1) * ROWS].T.astype(jnp.bfloat16)
        joined[group, yl, j, body] = merged[j, yl]

        def hand(source, target, peer):
            send(source, target, head_send.at[j], head_recv.at[j], peer).start()

        for y in range(ys):
            ctx = ctx_of(z, x, y, core)
            for g in (group, 1 - group):
                hand(
                    merged.at[j, y, pl.ds(0, MARGIN)],
                    joined.at[group, yl, j, pl.ds(MARGIN + ROWS, MARGIN)],
                    (before(ctx), g),
                )
                hand(
                    merged.at[j, y, pl.ds(ROWS - MARGIN, MARGIN)],
                    joined.at[group, yl, j, pl.ds(0, MARGIN)],
                    (after(ctx), g),
                )
        for peer, block in ((fellow, 1 - yl), (diagonal, 1 - yl), (partner, yl)):
            hand(merged.at[j, block], joined.at[group, yl, j, body], peer)

    def prepare(u):
        j, tile = tile_of(u)
        other, _ = z_peer(tile + 1)

        @pl.when(u < away)
        def _():
            drain(qq.at[j, pl.ds(other * ys, ys)], q_recv.at[j, other])

        @pl.when(tile == 0)
        def _():
            for step in range(xs):
                source = lax.rem(x + step, xs)
                drain(kv.at[j, pl.ds(slot(source, 1 - core, 0), ys)], sibling_recv.at[j, source])

        @pl.when(u == min(2, own - 1))
        def _():
            relay(own - 1)

        @pl.when(jnp.logical_and(tile == max(zs - 2, 0), j < own - 1))
        def _():
            forward(j + 1)

    even, odd = (product_even, peak_even), (product_odd, peak_odd)

    prepare(0)
    work(None, 0, *odd, *even)

    @pl.loop(0, tiles // 2 - 1)
    def _(pair):
        u = 2 * pair
        prepare(u + 1)
        work(u, u + 1, *even, *odd)
        prepare(u + 2)
        work(u + 1, u + 2, *odd, *even)

    for j in range(own - 2):
        combine(j)
    prepare(tiles - 1)
    work(tiles - 2, tiles - 1, *even, *odd)
    combine(own - 2)
    work(tiles - 1, None, *odd, *even)
    combine(own - 1)

    low = lax.broadcasted_iota(jnp.int32, (ROWS + 2 * MARGIN, 2 * HDIM), 1) < HDIM

    def project_out(j):
        drain(merged.at[pl.ds(0, 2)], head_recv.at[j])
        outs, slopes, weights = [], [], []
        for g in range(2):
            first = joined[g, 0, j].astype(jnp.float32)
            second = joined[g, 1, j].astype(jnp.float32)
            outs.append(jnp.where(low, first, pltpu.roll(second, HDIM, 1)))
            slopes.append(jnp.where(low, pltpu.roll(first, HDIM, 1), second))
            for y in range(ys):
                weights.append(wo_all[g, pl.ds((y * own + j) * HDIM, HDIM)])
        rows = jnp.concatenate(
            [jnp.concatenate(outs, axis=1), jnp.concatenate(slopes, axis=1)], axis=0
        )
        return jnp.dot(
            rows.astype(jnp.bfloat16),
            jnp.concatenate(weights, axis=0),
            preferred_element_type=jnp.float32,
        )

    wo_copy.wait()
    to_right.wait()
    to_left.wait()
    mixing = functools.reduce(jnp.add, [project_out(j) for j in range(own)])
    length = ROWS + 2 * MARGIN
    for which in range(2):
        mixed = inputs[which].astype(jnp.float32) + mixing[which * length : (which + 1) * length]
        wide[which] = mixed.astype(jnp.bfloat16).astype(jnp.float32)

    for load in loads[7:]:
        load.wait()
    taps = taps_ref.shape[0]
    reach = MARGIN - taps // 2
    for chunk in range(wide.shape[2] // 128):
        cols = slice(chunk * 128, (chunk + 1) * 128)
        weights = taps_ref[:, cols]
        filtered = []
        for which in range(2):
            total = jnp.zeros((ROWS, 128), jnp.float32)
            for phase in range(8):
                partial = None
                for tap in range(phase, taps, 8):
                    start = tap - phase
                    term = weights[tap : tap + 1] * wide[which, start : start + ROWS + 8, cols]
                    partial = term if partial is None else partial + term
                total = total + partial[phase + reach : phase + reach + ROWS]
            filtered.append(total)
        preact = filtered[0] + bias_ref[cols].reshape(1, -1)
        gating = 1.0 / (1.0 + jnp.exp(-preact))
        act[:ROWS, cols] = (preact * gating).astype(jnp.bfloat16)
        act[ROWS:, cols] = (
            gating * (1.0 + preact * (1.0 - gating)) * filtered[1]
        ).astype(jnp.bfloat16)

    total = jnp.dot(act[...], wm_ref[...], preferred_element_type=jnp.float32)
    own_cols = pl.ds(pl.multiple_of(group * half, 128), half)
    out_ref[0] = (wide[0, body, own_cols] + total[:ROWS]).astype(jnp.bfloat16)
    out_ref[1] = (wide[1, body, own_cols] + total[ROWS:]).astype(jnp.bfloat16)

    for j in range(own):
        drain(kv.at[j, pl.ds(0, 2 * ys * (xs - 1) + ys)], kv_send.at[j])
        if zs > 1:
            drain(qq.at[j, pl.ds(0, ys * (zs - 1))], q_send.at[j])
            drain(part_out.at[j, pl.ds(0, zs - 1)], part_send.at[j])
        drain(merged.at[pl.ds(0, 2)], head_send.at[j])


def shards(
    sizes,
    frames,
    tangent,
    norm_gain,
    query_weight,
    key_weight,
    value_weight,
    out_weight,
    conv_weight,
    conv_bias,
    mix_weight,
):
    zs, xs, ys, cs = sizes
    width, half = query_weight.shape
    heads = half // HDIM
    own = heads // ys
    nk = xs * cs * ys
    length = ROWS + 2 * MARGIN
    sem = pltpu.SemaphoreType.DMA
    hbm = pl.BlockSpec(memory_space=pl.ANY)
    vmem = pl.BlockSpec(memory_space=pltpu.VMEM)
    shape = jax.ShapeDtypeStruct((2, ROWS, half), jnp.bfloat16)
    operands = (
        frames,
        tangent,
        norm_gain,
        query_weight,
        key_weight,
        value_weight,
        out_weight,
        conv_weight,
        conv_bias,
        mix_weight,
    )
    part = (own, zs, 2 * HDIM + STAT, ys * ROWS)
    both = pl.pallas_call(
        functools.partial(kernel, sizes, heads),
        out_shape=shape,
        in_specs=[hbm] * len(operands),
        out_specs=vmem,
        scratch_shapes=[
            pltpu.VMEM((2, length, width), jnp.bfloat16),
            pltpu.VMEM((width,), jnp.float32),
            pltpu.VMEM((width, half), jnp.bfloat16),
            pltpu.VMEM((width, half), jnp.bfloat16),
            pltpu.VMEM((width, half), jnp.bfloat16),
            pltpu.VMEM((2, half, width), jnp.bfloat16),
            pltpu.VMEM(conv_weight.shape, jnp.float32),
            pltpu.VMEM((width,), jnp.float32),
            pltpu.VMEM((width, half), jnp.bfloat16),
            pltpu.VMEM((ys, own, 2, ROWS, 2 * HDIM), jnp.bfloat16),
            pltpu.VMEM((ys, own, 2 * HDIM, ROWS), jnp.bfloat16),
            pltpu.VMEM((own, nk, 2, ROWS, 2 * HDIM), jnp.bfloat16),
            pltpu.VMEM((own, zs * ys, 2 * HDIM, ROWS), jnp.bfloat16),
            pltpu.VMEM(part, jnp.bfloat16),
            pltpu.VMEM(part, jnp.bfloat16),
            pltpu.VMEM((own, ys, ROWS, 2 * HDIM), jnp.bfloat16),
            pltpu.VMEM((2, ys, own, length, 2 * HDIM), jnp.bfloat16),
            pltpu.VMEM((2, length, width), jnp.float32),
            pltpu.VMEM((2 * ROWS, width), jnp.bfloat16),
            pltpu.VMEM((nk * ROWS, 2 * ys * ROWS), jnp.float32),
            pltpu.VMEM((nk * ROWS, 2 * ys * ROWS), jnp.float32),
            pltpu.VMEM((nk * ROWS, 2 * ys * ROWS), jnp.bfloat16),
            pltpu.VMEM((8, ys * ROWS), jnp.float32),
            pltpu.VMEM((8, ys * ROWS), jnp.float32),
            sem((len(operands),)),
            sem((2, own)),
            sem((2, own)),
            sem((own,)),
            sem((own, xs, ys)),
            sem((own, xs)),
            sem((own,)),
            sem((own, zs)),
            sem((own,)),
            sem((own,)),
            sem((own,)),
            sem((own,)),
            sem((2,)),
            sem((4,)),
        ],
        compiler_params=pltpu.CompilerParams(
            collective_id=0, has_side_effects=True, vmem_limit_bytes=60 * 1024 * 1024
        ),
        name="block",
    )(*operands)
    return both[0], both[1]


def solution(mesh):
    sizes = FACTORS[mesh.shape["ctx"]]
    placed = (
        P("ctx", None),
        P("ctx", None),
        P(),
        P(None, "head"),
        P(None, "head"),
        P(None, "head"),
        P("head", None),
        P(),
        P(),
        P(None, "head"),
    )
    return jax.shard_map(
        functools.partial(shards, sizes),
        mesh=mesh,
        in_specs=placed,
        out_specs=(P("ctx", "head"), P("ctx", "head")),
        check_vma=False,
    )
```
